32 devices in a mesh: slab: 8 (over y, x, core), batch: 4 (over z).
Axes of the slice: x: 2, y: 2, z: 4, core: 2. Of those that a mesh axis runs over, the one named last changes fastest.
Arguments:
- volumes: bfloat16 [256, 2, 16384], P('slab', None, 'batch'), may hold values from -6 to 6
- band_weights: bfloat16 [2, 512, 32], P(None, 'slab'), may hold values from -1 to 1
- band_start: int32 [2, 512], P(None, 'slab'), may hold values from 0 to 224
- images: bfloat16 [1536, 16384], P('batch'), may hold values from -7 to 7
- noise_precision: float32 [1536], P('batch'), may hold values from 0.005004883 to 0.050048828
- log_prior: float32 [2, 512], P(None, 'slab'), may hold values from -4 to 4
Outputs:
- responsibilities: float32 [2, 512, 1536], P(None, 'slab', 'batch')
- log_evidence: float32 [1536], P('batch')
- backprojection: float32 [256, 2, 16384], P('slab', None, 'batch')
The draws below stay inside these ranges and needn't reach their ends.
All inputs are finite; a program needn't handle non-finite values.
Results may differ from the reference program's by a relative error of at most 0.0069.
Values may be sent and summed in bfloat16 or wider, within the bound.
No kernel may reach another device: no remote copies, remote signals or barrier semaphores. Data moves between devices by JAX's collectives and lax.ppermute only.
A program may use at most 64 MiB of HBM per device.

```python
import math
import jax
import jax.numpy as jnp
from jax import lax

K = 2
NZ = 256
P_SIZE = 16384
BAND = 32
O = 512
N = 1536


def plane_field(key):
    field_key = jax.random.fold_in(key, 11)
    field = jnp.clip(jax.random.normal(field_key, (NZ, K, P_SIZE), jnp.float32), -6.0, 6.0)
    return field.astype(jnp.bfloat16)


def band_starts(key):
    base = jax.random.randint(jax.random.fold_in(key, 21), (K * O,), 0, NZ - BAND + 1)
    first = jax.random.randint(jax.random.fold_in(key, 22), (), 0, K * O)
    offset = jax.random.randint(jax.random.fold_in(key, 23), (), 1, K * O)
    second = (first + offset) % (K * O)
    slots = jnp.arange(K * O, dtype=jnp.int32)
    base = jnp.where(slots == first, NZ - BAND, base)
    base = jnp.where(slots == second, 0, base)
    return base.reshape(K, O).astype(jnp.int32)


def band_taps(key):
    sign_bits = jax.random.randint(jax.random.fold_in(key, 31), (K, O, BAND), 0, 2)
    signs = (2 * sign_bits - 1).astype(jnp.float32)
    ranks = jax.random.randint(jax.random.fold_in(key, 32), (K, O, BAND), 0, 1 << 20)
    ranks = ranks * BAND + jnp.arange(BAND, dtype=jnp.int32)
    order = jnp.argsort(ranks, axis=-1, stable=True)
    levels = jnp.sqrt(2.0 * jnp.arange(BAND, dtype=jnp.float32) + 1.0) / BAND
    return (signs * jnp.take(levels, order)).astype(jnp.bfloat16)


def draw_volumes(key, part):
    return plane_field(key)


def draw_band_weights(key, part):
    return band_taps(key)


def draw_band_start(key, part):
    return band_starts(key)


def draw_images(key, part):
    field = plane_field(key).reshape(NZ * K, P_SIZE)
    taps = band_taps(key).astype(jnp.float32).reshape(K * O, BAND)
    starts = band_starts(key).reshape(K * O)
    owner = jnp.arange(K * O, dtype=jnp.int32) // O

    def add_tap(tap, total):
        rows_index = (starts + tap) * K + owner
        picked = jnp.take(field, rows_index, axis=0).astype(jnp.float32)
        weight = lax.dynamic_slice_in_dim(taps, tap, 1, 1)
        return total + weight * picked
    signal = lax.fori_loop(0, BAND, add_tap, jnp.zeros((K * O, P_SIZE), jnp.float32))
    chosen = jax.random.randint(jax.random.fold_in(key, 41), (N,), 0, K * O)
    strength = jnp.exp(jax.random.uniform(jax.random.fold_in(key, 42), (N,), jnp.float32, math.log(0.02), math.log(0.06)))
    noise_key = jax.random.fold_in(key, 43)
    noise = jnp.clip(jax.random.normal(noise_key, (N, P_SIZE), jnp.float32), -6.0, 6.0)
    images = strength[:, None] * jnp.take(signal, chosen, axis=0) + noise
    return images.astype(jnp.bfloat16)


def steps_of(rng, shape, shards, smallest, top_value):
    def one(position, shards_of):
        steps = jax.random.uniform(jax.random.fold_in(jax.random.fold_in(rng, 6), position), (shards_of,), jnp.float32, smallest / len(shards), top_value / len(shards))
        return jnp.repeat(jnp.exp(steps), shape[position] // shards_of).reshape((-1,) + (1,) * (len(shape) - position - 1))

    level = one(*shards[0])
    for cut in shards[1:]:
        level = level * one(*cut)
    return level


def gaussian(key, dims, spread, most, split=(), kind=jnp.bfloat16):
    entries = spread * jax.random.normal(key, dims, jnp.float32)
    if split:
        entries = entries * steps_of(key, dims, split, -0.22, 0.18)
    return jnp.clip(entries, -most, most).astype(kind)


def setup_inputs(seed: int = 0) -> dict:
    key_of = jax.random.split(jax.random.key(seed), 7)
    volumes = draw_volumes(jax.random.fold_in(key_of[6], 71), 0)
    band_weights = draw_band_weights(jax.random.fold_in(key_of[6], 71), 0)
    band_start = draw_band_start(jax.random.fold_in(key_of[6], 71), 0)
    images = draw_images(jax.random.fold_in(key_of[6], 71), 0)
    noise_precision = jnp.clip(jnp.exp(math.log(0.050048828) - 2.3025851 * jax.random.uniform(key_of[4], (N,), jnp.float32) ** steps_of(key_of[4], (N,), ((0, 4),), -0.2, 0.2)), 0.005004883, 0.050048828)
    log_prior = gaussian(key_of[5], (K, O), 1.0, 4.0, ((1, 8),), jnp.float32)
    return dict(volumes=volumes, band_weights=band_weights, band_start=band_start, images=images, noise_precision=noise_precision, log_prior=log_prior)


def build_slice(band_weights, band_start, planes):
    offsets = planes[None, None, :] - band_start[:, :, None]
    taps = jnp.arange(BAND, dtype=jnp.int32)
    hits = offsets[..., None] == taps
    values = jnp.where(hits, band_weights.astype(jnp.float32)[:, :, None, :], jnp.float32(0.0))
    return jnp.sum(values, axis=-1)


def reference(volumes, band_weights, band_start, images, noise_precision, log_prior):
    slice_full = build_slice(band_weights, band_start, jnp.arange(NZ, dtype=jnp.int32))
    projection = jnp.einsum("koz,zkp->okp", slice_full, volumes.astype(jnp.float32)).astype(jnp.bfloat16)
    wide = projection.astype(jnp.float32)
    energy = jnp.sum(wide * wide, axis=2)
    flat = projection.reshape(O * K, P_SIZE)
    inner = jnp.dot(flat, images.T, preferred_element_type=jnp.float32).reshape(O, K, N)
    inner = jnp.transpose(inner, (1, 0, 2))
    score = noise_precision[None, None, :] * (inner - 0.5 * energy.T[:, :, None]) + log_prior[:, :, None]
    top = jnp.max(score, axis=(0, 1))
    total = jnp.sum(jnp.exp(score - top[None, None, :]), axis=(0, 1))
    log_evidence = top + jnp.log(total)
    responsibilities = jnp.exp(score - log_evidence[None, None, :])
    weights = responsibilities.astype(jnp.bfloat16).reshape(K * O, N)
    image_sum = jnp.dot(images.T, weights.T, preferred_element_type=jnp.float32).reshape(P_SIZE, K, O)
    backprojection = jnp.einsum("koz,pko->zkp", slice_full, image_sum, precision=lax.Precision.HIGHEST)
    return responsibilities, log_evidence, backprojection
```

```python
import jax
import jax.numpy as jnp
import numpy as np
from jax import lax
from jax.sharding import PartitionSpec as P


def build_slice(band_weights, band_start, planes):
    offsets = planes[None, None, :] - band_start[:, :, None]
    taps = jnp.arange(band_weights.shape[2], dtype=jnp.int32)
    hits = offsets[..., None] == taps
    values = jnp.where(hits, band_weights[:, :, None, :], jnp.float32(0.0))
    return jnp.sum(values, axis=-1)


def shifted(value, axis, step):
    size = lax.axis_size(axis)
    return lax.ppermute(value, axis, [(i, (i + step) % size) for i in range(size)])


def folded_ring(size):
    return list(range(0, size, 2)) + list(range(size - 1 - size % 2, 0, -2))


def paired(value, masks):
    size = lax.axis_size("slab")
    return lax.ppermute(value, "slab", [(i, i ^ masks[i % 2]) for i in range(size)])


def gather_blocks(block):
    size = lax.axis_size("slab")
    bits = [1 << i for i in range(1, size.bit_length() - 1)]
    held = block[None]
    for up, down in zip(bits, reversed(bits)):
        held = jnp.concatenate([held, paired(held, (up, down))])
    return held, paired(held, (1, 1))


def held_masks(size, core):
    bits = [1 << i for i in range(1, size.bit_length() - 1)]
    masks = [0]
    for bit in bits if core == 0 else reversed(bits):
        masks = masks + [mask ^ bit for mask in masks]
    return masks


def local(volumes, band_weights, band_start, images, noise_precision, log_prior):
    planes, classes, block = volumes.shape
    slabs, batches = lax.axis_size("slab"), lax.axis_size("batch")
    slab, batch = lax.axis_index("slab"), lax.axis_index("batch")
    all_planes = planes * slabs
    strip = block // slabs
    own_o = band_weights.shape[1]
    particles = images.shape[0]
    rows = particles // slabs
    f32, bf16 = jnp.float32, jnp.bfloat16

    def fetch(step):
        column = lax.rem(batch + step, batches) * block
        part = lax.dynamic_slice(images, (slab * rows, column), (rows, block))
        return shifted(part, "batch", step)

    fetched = {step: fetch(step) for step in range(1, batches)}

    strips = lax.all_to_all(
        jnp.transpose(volumes, (1, 0, 2)), "slab", split_axis=2, concat_axis=1, tiled=True
    )
    table = jnp.concatenate(
        [
            band_weights.astype(f32),
            band_start.astype(f32)[:, :, None],
        ],
        axis=2,
    )
    table = lax.all_gather(table, "slab", axis=1, tiled=True)
    all_slices = build_slice(
        table[:, :, :-1], table[:, :, -1].astype(jnp.int32), jnp.arange(all_planes, dtype=jnp.int32)
    ).astype(bf16)

    ring = folded_ring(batches)
    place_of = np.argsort(ring)
    hops = [(ring[i], ring[(i + 1) % batches]) for i in range(batches)]
    place = jnp.asarray(place_of, jnp.int32)[batch]
    inner = 0.0
    energy = 0.0
    for step in range(batches):
        owner = jnp.asarray(ring, jnp.int32)[lax.rem(place + batches - step, batches)]
        following = lax.ppermute(strips, "batch", hops) if step < batches - 1 else None
        projection = jnp.einsum(
            "koz,kzp->kop", all_slices, strips, preferred_element_type=f32
        ).astype(bf16)
        columns = lax.dynamic_slice(
            images, (0, owner * block + slab * strip), (particles, strip)
        )
        inner = inner + jnp.einsum("kop,np->kon", projection, columns, preferred_element_type=f32)
        wide = projection.astype(f32)
        energy = energy + jnp.sum(wide * wide, axis=2)
        strips = following

    partial = inner - 0.5 * energy[:, :, None]
    partial = partial.reshape(classes, slabs, own_o, particles)
    partial = lax.all_to_all(partial, "slab", split_axis=1, concat_axis=1, tiled=True)
    score = noise_precision[None, None, :] * jnp.sum(partial, axis=1) + log_prior[:, :, None]

    own_top = jnp.max(score, axis=(0, 1))
    shifted_exp = jnp.exp(score - own_top)
    own_total = jnp.sum(shifted_exp, axis=(0, 1))
    tops, totals = lax.all_gather((own_top, own_total), "slab")
    exps = lax.all_gather(shifted_exp.astype(bf16), "slab")
    top = jnp.max(tops, axis=0)
    total = jnp.sum(totals * jnp.exp(tops - top), axis=0)
    log_evidence = top + jnp.log(total)
    responsibilities = jnp.exp(score - log_evidence)
    scale = jnp.exp(tops - log_evidence)
    weights = (exps.astype(f32) * scale[:, None, None, :]).astype(bf16)

    own_slices = lax.dynamic_slice_in_dim(all_slices, slab * planes, planes, axis=2)
    own_slices = own_slices.reshape(classes, slabs, own_o, planes)
    inserted = jnp.einsum("ksoz,skon->nkz", own_slices, weights, preferred_element_type=f32)
    inserted = inserted.astype(bf16).reshape(particles, classes * planes)

    def back(values, pixels):
        return jnp.einsum("nz,np->zp", values, pixels, preferred_element_type=f32)

    result = back(inserted, lax.dynamic_slice_in_dim(images, batch * block, block, axis=1))

    by_rows = inserted.reshape(slabs, rows, classes * planes)
    orders = jnp.asarray([held_masks(slabs, core) for core in (0, 1)], jnp.int32)
    order = slab ^ orders[slab % 2]
    order = jnp.concatenate([order, slab ^ 1 ^ orders[1 - slab % 2]])
    by_rows = jnp.take(by_rows, order, axis=0).reshape(2, particles // 2, classes * planes)
    for step in range(1, batches):
        mine, other = gather_blocks(fetched[step])
        there = shifted(by_rows, "batch", step)
        result = result + back(there[0], mine.reshape(particles // 2, block))
        result = result + back(there[1], other.reshape(particles // 2, block))
    backprojection = jnp.transpose(result.reshape(classes, planes, block), (1, 0, 2))
    return (responsibilities, log_evidence, backprojection)


def solution(mesh):
    in_specs = (
        P("slab", None, "batch"),
        P(None, "slab", None),
        P(None, "slab"),
        P("batch", None),
        P("batch"),
        P(None, "slab"),
    )
    out_specs = (P(None, "slab", "batch"), P("batch"), P("slab", None, "batch"))
    return jax.shard_map(local, mesh=mesh, in_specs=in_specs, out_specs=out_specs, check_vma=False)
```

```python
import jax
import jax.numpy as jnp
from jax import lax
from jax.experimental import pallas as pl
from jax.experimental.pallas import tpu as pltpu
from jax.sharding import PartitionSpec as P

f32, bf16 = jnp.float32, jnp.bfloat16
params = pltpu.CompilerParams(vmem_limit_bytes=60 << 20)


def after(value, *others):
    return lax.optimization_barrier((value,) + others)[0]


def turned_taps(table, classes, own_o):
    depth, group = table.shape
    taps = depth - 5
    period = taps * classes
    tap = lax.broadcasted_iota(jnp.int32, (period, taps), 1)
    row = lax.broadcasted_iota(jnp.int32, (period, taps), 0)
    spread = jnp.where(row // classes == tap, 1.0, 0.0).astype(bf16)
    base = jnp.dot(spread, table[:taps].astype(bf16), preferred_element_type=f32)
    start = 128.0 * table[taps : taps + 1] + table[taps + 1 : taps + 2]
    start = start.astype(jnp.int32)
    for bit in range((taps - 1).bit_length()):
        moved = pltpu.roll(base, classes << bit, 0)
        base = jnp.where(start & (1 << bit) != 0, moved, base)
    row = lax.broadcasted_iota(jnp.int32, (period, group), 0)
    column = lax.broadcasted_iota(jnp.int32, (period, group), 1)
    return jnp.where(row % classes == column // own_o, base, 0.0), start


def window(turned, slab, planes, taps, classes):
    base, start = turned
    if planes % taps == 0:
        rows = jnp.concatenate([base] * (planes // taps))
    else:
        width = planes * classes
        rows = base[:width]
        for i in range(1, taps // planes):
            rows = jnp.where(
                slab % (taps // planes) == i, base[i * width : (i + 1) * width], rows
            )
    row = lax.broadcasted_iota(jnp.int32, rows.shape, 0)
    place = slab * planes + row // classes - start
    return jnp.where(jnp.logical_and(place >= 0, place < taps), rows, 0.0)


def even_first(one, two, core):
    return [jnp.where(core == 0, one, two), jnp.where(core == 0, two, one)]


def window_kernel(planes, classes, own_o, order_ref, tables_ref, out_ref):
    group = tables_ref.shape[2]
    taps = tables_ref.shape[1] - 5
    width = planes * classes
    core = order_ref[0] & 1
    for i in range(out_ref.shape[0]):
        tables = even_first(tables_ref[2 * i], tables_ref[2 * i + 1], core)
        for side, table in enumerate(tables):
            turned = turned_taps(table, classes, own_o)
            for part, slab in enumerate((order_ref[0], order_ref[0] ^ 1)):
                rows = window(turned, slab, planes, taps, classes)
                out_ref[
                    i, part * width : (part + 1) * width, side * group : (side + 1) * group
                ] = rows.astype(bf16)


def window_slices(order, tables, planes, classes, own_o):
    slabs, _, group = tables.shape
    vmem = pl.BlockSpec(memory_space=pltpu.VMEM)
    return pl.pallas_call(
        lambda *refs: window_kernel(planes, classes, own_o, *refs),
        in_specs=[pl.BlockSpec(memory_space=pltpu.SMEM), vmem],
        out_specs=vmem,
        out_shape=jax.ShapeDtypeStruct((slabs // 2, 2 * planes * classes, 2 * group), bf16),
        compiler_params=params,
        name="window_slices",
    )(order, tables)


def shifted(value, axis, step):
    size = lax.axis_size(axis)
    return lax.ppermute(value, axis, [(i, (i + step) % size) for i in range(size)])


def paired(value, masks):
    size = lax.axis_size("slab")
    return lax.ppermute(value, "slab", [(i, i ^ masks[i % 2]) for i in range(size)])


def mask_steps(size):
    bits = [1 << i for i in range(1, size.bit_length() - 1)]
    return list(zip(bits, reversed(bits)))


def held_masks(size, core):
    masks = [0]
    for step in mask_steps(size):
        masks = masks + [mask ^ step[core] for mask in masks]
    return masks


def block_orders():
    size = lax.axis_size("slab")
    slab = lax.axis_index("slab")
    core = slab & 1
    masks = list(zip(held_masks(size, 0), held_masks(size, 1)))
    own = [slab ^ (even + core * (odd - even)) for even, odd in masks]
    other = [slab ^ 1 ^ (odd + core * (even - odd)) for even, odd in masks]
    return own, other


def chip_places(parity):
    chips = lax.axis_size("slab") // 2
    chip = lax.axis_index("slab") // 2
    depth = chips.bit_length() - 1
    places = []
    for other in range(chips):
        apart = chip ^ other
        turned = sum(((apart >> i) & 1) << (depth - 1 - i) for i in range(depth))
        places.append(apart + parity * (turned - apart))
    return places


def spread_start(block):
    return [block] + [paired(block, step) for step in mask_steps(lax.axis_size("slab"))]


def spread_end(blocks):
    held = blocks[:2]
    for step, block in zip(mask_steps(lax.axis_size("slab"))[1:], blocks[2:]):
        held = held + [block] + [paired(each, step) for each in held[1:]]
    return held


def sum_images_kernel(*refs):
    count = refs[-1].shape[0]
    values = [ref for ref in refs[:-2] if ref.shape[1] == 2 * count]
    pixels = refs[len(values) : -2]
    rows = values[0].shape[0]
    contract = (((0,), (0,)), ((), ()))
    total = 0.0
    place = 0
    for pixel in pixels:
        for top in range(0, pixel.shape[0], rows):
            total += lax.dot_general(
                values[place][...],
                pixel[top : top + rows],
                contract,
                preferred_element_type=f32,
            )
            place += 1
    refs[-2][...] = total[:count]
    refs[-1][...] = total[count:]


def sum_images(values, pixels):
    rows, width = values[0].shape
    block = pixels[0].shape[1]
    tile = min(block, 2048)
    half = jax.ShapeDtypeStruct((width // 2, block), f32)
    return pl.pallas_call(
        sum_images_kernel,
        grid=(block // tile,),
        in_specs=[pl.BlockSpec((rows, width), lambda i: (0, 0))] * len(values)
        + [pl.BlockSpec((pixel.shape[0], tile), lambda i: (0, i)) for pixel in pixels],
        out_specs=[pl.BlockSpec((width // 2, tile), lambda i: (0, i))] * 2,
        out_shape=[half, half],
        compiler_params=params,
        name="sum_images",
    )(*values, *pixels)


def add_parts_kernel(one_ref, two_ref, out_ref):
    total = one_ref[...] + two_ref[...]
    out_ref[...] = total.reshape(out_ref.shape)


def add_parts(one, two, classes):
    width, block = one.shape
    tile = min(block, 4096)
    part = pl.BlockSpec((width, tile), lambda i: (0, i))
    return pl.pallas_call(
        add_parts_kernel,
        grid=(block // tile,),
        in_specs=[part] * 2,
        out_specs=pl.BlockSpec((width // classes, classes, tile), lambda i: (0, 0, i)),
        out_shape=jax.ShapeDtypeStruct((width // classes, classes, block), f32),
        compiler_params=params,
        name="add_parts",
    )(one, two)


def project_kernel(planes, classes, own_o, depth, order_ref, *refs):
    pieces, (out_ref, prior_ref, tables_ref) = refs[:-3], refs[-3:]
    width = planes * classes
    group = classes * own_o
    taps = depth - 5
    block = pieces[0].shape[1]
    core = order_ref[0] & 1
    lines = -(-depth * group // block)
    for i, piece in enumerate(pieces):
        flat = piece[2 * width :].astype(f32)
        for side in range(2):
            table = []
            for line in range(depth):
                row, column = divmod(line * group, block)
                row += side * lines
                table.append(flat[row : row + 1, column : column + group])
            tables_ref[2 * i + side] = jnp.concatenate(table)
    chip = even_first(tables_ref[0], tables_ref[1], core)
    prior = [jnp.sum(table[taps + 2 :], axis=0, keepdims=True) for table in chip]
    prior_ref[...] = jnp.concatenate(prior, axis=1)
    turned = [turned_taps(table, classes, own_o) for table in chip]
    slices = []
    for i in range(len(pieces)):
        for slab in (order_ref[i], order_ref[i] ^ 1):
            parts = [window(one, slab, planes, taps, classes) for one in turned]
            slices.append(jnp.concatenate(parts, axis=1))
    slices = jnp.concatenate(slices).T.astype(bf16)
    tile = min(block, 512)

    def some(i, energy):
        columns = pl.ds(pl.multiple_of(i * tile, tile), tile)
        stack = jnp.concatenate([piece[: 2 * width, columns] for piece in pieces])
        projection = jnp.dot(slices, stack, preferred_element_type=f32)
        projection = projection.astype(bf16).astype(f32).T
        out_ref[columns] = projection.astype(bf16)
        return energy + jnp.sum(projection * projection, axis=0, keepdims=True)

    energy = lax.fori_loop(0, block // tile, some, jnp.zeros((1, 2 * group), f32))
    high = energy.astype(bf16).astype(f32)
    middle = (energy - high).astype(bf16).astype(f32)
    parts = [high, middle, energy - high - middle, jnp.zeros((13, 2 * group), f32)]
    parts = jnp.concatenate(parts)
    out_ref[block:] = parts.astype(bf16)


def project(order, pieces, planes, classes, own_o, depth):
    block = pieces[0].shape[1]
    group = classes * own_o
    vmem = pl.BlockSpec(memory_space=pltpu.VMEM)
    return pl.pallas_call(
        lambda *refs: project_kernel(planes, classes, own_o, depth, *refs),
        in_specs=[pl.BlockSpec(memory_space=pltpu.SMEM)] + [vmem] * len(pieces),
        out_specs=[vmem] * 3,
        out_shape=[
            jax.ShapeDtypeStruct((block + 16, 2 * group), bf16),
            jax.ShapeDtypeStruct((1, 2 * group), f32),
            jax.ShapeDtypeStruct((2 * len(pieces), depth, group), f32),
        ],
        compiler_params=params,
        name="project",
    )(order, *pieces)


def match_kernel(count, order_ref, mine_ref, theirs_ref, *refs):
    pieces, out_ref, pixels_ref = refs[:-2], refs[-2], refs[-1]
    rows = pieces[0].shape[0] // count
    half = mine_ref.shape[0] - 16
    core = order_ref[0] & 1
    wide = [piece[...] if rows % 16 == 0 else piece[...].astype(f32) for piece in pieces]
    stack = [piece[i * rows : (i + 1) * rows] for i in range(count) for piece in wide]
    pixels_ref[...] = jnp.concatenate(stack).astype(bf16)
    squares = mine_ref[half:].astype(f32) + theirs_ref[half:].astype(f32)
    energy = jnp.sum(squares, axis=0, keepdims=True)
    total = -0.5 * energy
    for side, projection in ((core, mine_ref), (1 - core, theirs_ref)):
        columns = pl.ds(pl.multiple_of(side * half, half), half)
        total += jnp.dot(pixels_ref[:, columns], projection[:half], preferred_element_type=f32)
    out_ref[...] = total.reshape(out_ref.shape)


def match(order, mine, theirs, pieces, count):
    rows, block = pieces[0].shape
    rows_all = rows * len(pieces)
    columns = mine.shape[1]
    vmem = pl.BlockSpec(memory_space=pltpu.VMEM)
    return pl.pallas_call(
        lambda *refs: match_kernel(count, *refs),
        in_specs=[pl.BlockSpec(memory_space=pltpu.SMEM)] + [vmem] * (2 + len(pieces)),
        out_specs=[vmem] * 2,
        out_shape=[
            jax.ShapeDtypeStruct((count, rows_all // count, columns), f32),
            jax.ShapeDtypeStruct((rows_all, block), bf16),
        ],
        compiler_params=params,
        name="match",
    )(order, mine, theirs, *pieces)


def pick(blocks, order):
    return jnp.concatenate([lax.dynamic_slice_in_dim(blocks, i, 1) for i in order])


def in_three(value):
    high = lax.reduce_precision(value, 8, 7)
    rest = value - high
    middle = lax.reduce_precision(rest, 8, 7)
    return [part.astype(bf16) for part in (high, middle, rest - middle)]


def local(volumes, band_weights, band_start, images, noise_precision, log_prior):
    planes, classes, block = volumes.shape
    slabs, batches = lax.axis_size("slab"), lax.axis_size("batch")
    slab, batch = lax.axis_index("slab"), lax.axis_index("batch")
    core = slab & 1
    chips = slabs // 2
    own_o, taps = band_weights.shape[1:]
    particles = images.shape[0]
    rows = particles // slabs
    width = planes * classes
    group = classes * own_o
    own_order, other_order = block_orders()

    def fetch(step, *earlier):
        column = lax.rem(batch + step, batches) * block
        part = lax.dynamic_slice(images, (slab * rows, column), (rows, block))
        return shifted(after(part, *earlier) if earlier else part, "batch", step)

    half = batches // 2
    steps = [step for step in range(1, batches) if step != half]
    fetched = [fetch(step) for step in steps]
    last = fetch(half)

    coarse = band_start // 128
    table = jnp.concatenate(
        [
            band_weights.reshape(group, taps).T,
            jnp.stack([coarse, band_start - 128 * coarse]).reshape(2, group).astype(bf16),
            jnp.stack(in_three(log_prior)).reshape(3, group),
        ]
    )
    depth = table.shape[0]
    side = block // 2
    extra = -(-table.size // side)
    table = jnp.pad(table.reshape(-1), (0, extra * side - table.size)).reshape(extra, side)
    flat = volumes.reshape(width, block)
    mine = lax.dynamic_slice_in_dim(flat, core * side, side, axis=1)
    give = lax.dynamic_slice_in_dim(flat, (1 - core) * side, side, axis=1)
    theirs = paired(jnp.concatenate([give, table]), (1, 1))
    shard = jnp.concatenate([mine, theirs[:width], table, theirs[width:]])
    shards = spread_end(spread_start(shard))
    near = spread_start(after(jnp.concatenate(fetched), *shards[1:])) if steps else []
    order = jnp.stack(own_order)
    mine, prior, tables = project(order, shards, planes, classes, own_o, depth)
    mine = after(mine, last, *near)
    theirs = paired(mine, (1, 1))

    own = [lax.dynamic_slice(images, (i * rows, batch * block), (rows, block)) for i in own_order]
    total, pixels = match(order, mine, theirs, own, 1)
    total = total[0]
    pixels = [pixels]
    if steps:
        parts, pixel = match(order, mine, theirs, spread_end(near), len(steps))
        pixels.append(pixel)
        for step, part in zip(steps, parts):
            total = total + shifted(part, "batch", -step)
    part, pixel = match(order, mine, theirs, spread_end(spread_start(last)), 1)
    pixels.append(pixel)
    total = total + shifted(part[0], "batch", -half)
    total = total.reshape(chips, rows, 2 * group)

    def by_rows(blocks):
        return pick(blocks, chip_places(core))

    noise = lax.dynamic_index_in_dim(noise_precision.reshape(chips, 2, rows), core, 1, False)
    score = noise[:, :, None] * by_rows(total) + prior
    own_top = jnp.max(score, axis=2)
    shifted_exp = jnp.exp(score - own_top[:, :, None])
    own_total = jnp.sum(shifted_exp, axis=2)
    count = chips * rows
    lines = -(-count // (2 * group))
    sides = jnp.stack(in_three(own_top.reshape(count)) + in_three(own_total.reshape(count)))
    sides = jnp.pad(sides, ((0, 0), (0, lines * 2 * group - count))).reshape(-1, 2 * group)
    packed = jnp.concatenate([shifted_exp.astype(bf16).reshape(count, 2 * group), sides])
    mates = [list(range(parity, slabs, 2)) for parity in (0, 1)]
    packed = lax.all_gather(packed, "slab", axis_index_groups=mates)
    exps = packed[:, :count]
    sides = packed[:, count:].reshape(chips, 6, lines * 2 * group)[:, :, :count].astype(f32)
    tops = sides[:, 0] + sides[:, 1] + sides[:, 2]
    totals = sides[:, 3] + sides[:, 4] + sides[:, 5]
    top = jnp.max(tops, axis=0)
    log_evidence = top + jnp.log(jnp.sum(totals * jnp.exp(tops - top), axis=0))
    scale = jnp.exp(tops - log_evidence)
    weights = (exps.astype(f32) * scale[:, :, None]).astype(bf16)

    chip_order = [i // 2 for i in own_order]
    both = pick(window_slices(order, tables, planes, classes, own_o), chip_places(core))
    inserted = jnp.einsum("qzo,qno->nz", both, weights, preferred_element_type=f32).astype(bf16)
    inserted = pick(inserted.reshape(chips, rows, 2 * width), chip_order)
    inserted = inserted.reshape(count, 2 * width)
    there = [inserted] + [shifted(inserted, "batch", step) for step in steps + [half]]

    responsibilities = jnp.exp(score.reshape(count, 2 * group) - log_evidence[:, None])
    lines = -(-count // group)
    evidence = jnp.pad(log_evidence, (0, lines * group - count)).reshape(lines, group)
    halves = even_first(responsibilities[:, :group], responsibilities[:, group:], core)
    mine = jnp.concatenate([halves[0], evidence])
    theirs = paired(jnp.concatenate([halves[1], evidence]), (1, 1))

    def in_order(one, two):
        return jnp.stack(even_first(one, two, core), axis=1)

    responsibilities = in_order(
        mine[:count].reshape(chips, rows, group), theirs[:count].reshape(chips, rows, group)
    ).reshape(particles, group)
    evidence = [each[count:].reshape(-1)[:count].reshape(chips, rows) for each in (mine, theirs)]
    log_evidence = in_order(*evidence).reshape(particles)

    there[0] = after(there[0], theirs)
    keep, give = sum_images(there, pixels)
    backprojection = add_parts(keep, paired(give, (1, 1)), classes)
    return (
        responsibilities.T.reshape(classes, own_o, particles),
        log_evidence,
        backprojection,
    )


def solution(mesh):
    in_specs = (
        P("slab", None, "batch"),
        P(None, "slab", None),
        P(None, "slab"),
        P("batch", None),
        P("batch"),
        P(None, "slab"),
    )
    out_specs = (P(None, "slab", "batch"), P("batch"), P("slab", None, "batch"))
    return jax.shard_map(local, mesh=mesh, in_specs=in_specs, out_specs=out_specs, check_vma=False)
```

```python
import jax
import jax.numpy as jnp
from jax import lax
from jax.experimental import pallas as pl
from jax.experimental.pallas import tpu as pltpu
from jax.sharding import PartitionSpec as P

f32, bf16 = jnp.float32, jnp.bfloat16
params = pltpu.CompilerParams(vmem_limit_bytes=60 << 20)


def cost(flops, *arrays):
    size = sum(array.size * array.dtype.itemsize for array in arrays)
    return pl.CostEstimate(flops=flops, bytes_accessed=size, transcendentals=0)


def after(value, *others):
    return lax.optimization_barrier((value,) + others)[0]


def turned_taps(table, classes, own_o):
    depth, group = table.shape
    taps = depth - 5
    period = taps * classes
    tap = lax.broadcasted_iota(jnp.int32, (period, taps), 1)
    row = lax.broadcasted_iota(jnp.int32, (period, taps), 0)
    spread = jnp.where(row // classes == tap, 1.0, 0.0).astype(bf16)
    base = jnp.dot(spread, table[:taps].astype(bf16), preferred_element_type=f32)
    start = 128.0 * table[taps : taps + 1] + table[taps + 1 : taps + 2]
    start = start.astype(jnp.int32)
    for bit in range((taps - 1).bit_length()):
        moved = pltpu.roll(base, classes << bit, 0)
        base = jnp.where(start & (1 << bit) != 0, moved, base)
    row = lax.broadcasted_iota(jnp.int32, (period, group), 0)
    column = lax.broadcasted_iota(jnp.int32, (period, group), 1)
    return jnp.where(row % classes == column // own_o, base, 0.0), start


def window(turned, slab, planes, taps, classes):
    base, start = turned
    if planes % taps == 0:
        rows = jnp.concatenate([base] * (planes // taps))
    else:
        width = planes * classes
        rows = base[:width]
        for i in range(1, taps // planes):
            rows = jnp.where(
                slab % (taps // planes) == i, base[i * width : (i + 1) * width], rows
            )
    row = lax.broadcasted_iota(jnp.int32, rows.shape, 0)
    place = slab * planes + row // classes - start
    return jnp.where(jnp.logical_and(place >= 0, place < taps), rows, 0.0)


def even_first(one, two, core):
    return [jnp.where(core == 0, one, two), jnp.where(core == 0, two, one)]


def window_kernel(planes, classes, own_o, order_ref, tables_ref, out_ref):
    group = tables_ref.shape[2]
    taps = tables_ref.shape[1] - 5
    width = planes * classes
    core = order_ref[0] & 1
    for i in range(out_ref.shape[0]):
        tables = even_first(tables_ref[2 * i], tables_ref[2 * i + 1], core)
        for side, table in enumerate(tables):
            turned = turned_taps(table, classes, own_o)
            for part, slab in enumerate((order_ref[0], order_ref[0] ^ 1)):
                rows = window(turned, slab, planes, taps, classes)
                out_ref[
                    i, part * width : (part + 1) * width, side * group : (side + 1) * group
                ] = rows.astype(bf16)


def window_slices(order, tables, planes, classes, own_o):
    slabs, _, group = tables.shape
    vmem = pl.BlockSpec(memory_space=pltpu.VMEM)
    return pl.pallas_call(
        lambda *refs: window_kernel(planes, classes, own_o, *refs),
        in_specs=[pl.BlockSpec(memory_space=pltpu.SMEM), vmem],
        out_specs=vmem,
        out_shape=jax.ShapeDtypeStruct((slabs // 2, 2 * planes * classes, 2 * group), bf16),
        compiler_params=params,
        cost_estimate=cost(0, tables),
        name="window_slices",
    )(order, tables)


def shifted(value, axis, step):
    size = lax.axis_size(axis)
    return lax.ppermute(value, axis, [(i, (i + step) % size) for i in range(size)])


def paired(value, masks):
    size = lax.axis_size("slab")
    return lax.ppermute(value, "slab", [(i, i ^ masks[i % 2]) for i in range(size)])


def mask_steps(size):
    bits = [1 << i for i in range(1, size.bit_length() - 1)]
    return list(zip(bits, reversed(bits)))


def held_masks(size, core):
    masks = [0]
    for step in mask_steps(size):
        masks = masks + [mask ^ step[core] for mask in masks]
    return masks


def block_orders():
    size = lax.axis_size("slab")
    slab = lax.axis_index("slab")
    core = slab & 1
    masks = list(zip(held_masks(size, 0), held_masks(size, 1)))
    own = [slab ^ (even + core * (odd - even)) for even, odd in masks]
    other = [slab ^ 1 ^ (odd + core * (even - odd)) for even, odd in masks]
    return own, other


def chip_places(parity):
    chips = lax.axis_size("slab") // 2
    chip = lax.axis_index("slab") // 2
    depth = chips.bit_length() - 1
    places = []
    for other in range(chips):
        apart = chip ^ other
        turned = sum(((apart >> i) & 1) << (depth - 1 - i) for i in range(depth))
        places.append(apart + parity * (turned - apart))
    return places


def spread_start(block):
    return [block] + [paired(block, step) for step in mask_steps(lax.axis_size("slab"))]


def spread_end(blocks):
    held = blocks[:2]
    for step, block in zip(mask_steps(lax.axis_size("slab"))[1:], blocks[2:]):
        held = held + [block] + [paired(each, step) for each in held[1:]]
    return held


def sum_images_kernel(*refs):
    count = refs[-1].shape[0]
    values = [ref for ref in refs[:-2] if ref.shape[1] == 2 * count]
    pixels = refs[len(values) : -2]
    rows = values[0].shape[0]
    contract = (((0,), (0,)), ((), ()))
    total = 0.0
    place = 0
    for pixel in pixels:
        for top in range(0, pixel.shape[0], rows):
            total += lax.dot_general(
                values[place][...],
                pixel[top : top + rows],
                contract,
                preferred_element_type=f32,
            )
            place += 1
    refs[-2][...] = total[:count]
    refs[-1][...] = total[count:].astype(bf16)


def sum_images(values, pixels):
    rows, width = values[0].shape
    block = pixels[0].shape[1]
    tile = min(block, 2048)
    half = jax.ShapeDtypeStruct((width // 2, block), f32)
    return pl.pallas_call(
        sum_images_kernel,
        grid=(block // tile,),
        in_specs=[pl.BlockSpec((rows, width), lambda i: (0, 0))] * len(values)
        + [pl.BlockSpec((pixel.shape[0], tile), lambda i: (0, i)) for pixel in pixels],
        out_specs=[pl.BlockSpec((width // 2, tile), lambda i: (0, i))] * 2,
        out_shape=[half, jax.ShapeDtypeStruct((width // 2, block), bf16)],
        compiler_params=params,
        cost_estimate=cost(2 * rows * len(values) * width * block, *values, *pixels),
        name="sum_images",
    )(*values, *pixels)


def add_parts_kernel(one_ref, two_ref, out_ref):
    total = one_ref[...] + two_ref[...]
    out_ref[...] = total.reshape(out_ref.shape)


def add_parts(one, two, classes):
    width, block = one.shape
    tile = min(block, 4096)
    part = pl.BlockSpec((width, tile), lambda i: (0, i))
    return pl.pallas_call(
        add_parts_kernel,
        grid=(block // tile,),
        in_specs=[part] * 2,
        out_specs=pl.BlockSpec((width // classes, classes, tile), lambda i: (0, 0, i)),
        out_shape=jax.ShapeDtypeStruct((width // classes, classes, block), f32),
        compiler_params=params,
        cost_estimate=cost(2 * width * block, one, two, one),
        name="add_parts",
    )(one, two)


def project_kernel(planes, classes, own_o, depth, order_ref, *refs):
    pieces, (out_ref, prior_ref, tables_ref) = refs[:-3], refs[-3:]
    width = planes * classes
    group = classes * own_o
    taps = depth - 5
    block = pieces[0].shape[1]
    core = order_ref[0] & 1
    lines = -(-depth * group // block)
    for i, piece in enumerate(pieces):
        flat = piece[2 * width :].astype(f32)
        for side in range(2):
            table = []
            for line in range(depth):
                row, column = divmod(line * group, block)
                row += side * lines
                table.append(flat[row : row + 1, column : column + group])
            tables_ref[2 * i + side] = jnp.concatenate(table)
    chip = even_first(tables_ref[0], tables_ref[1], core)
    prior = [jnp.sum(table[taps + 2 :], axis=0, keepdims=True) for table in chip]
    prior_ref[...] = jnp.concatenate(prior, axis=1)
    turned = [turned_taps(table, classes, own_o) for table in chip]
    slices = []
    for i in range(len(pieces)):
        for slab in (order_ref[i], order_ref[i] ^ 1):
            parts = [window(one, slab, planes, taps, classes) for one in turned]
            slices.append(jnp.concatenate(parts, axis=1))
    slices = jnp.concatenate(slices).T.astype(bf16)
    tile = min(block, 512)

    def some(i, energy):
        columns = pl.ds(pl.multiple_of(i * tile, tile), tile)
        stack = jnp.concatenate([piece[: 2 * width, columns] for piece in pieces])
        projection = jnp.dot(slices, stack, preferred_element_type=f32)
        projection = projection.astype(bf16).astype(f32).T
        out_ref[columns] = projection.astype(bf16)
        return energy + jnp.sum(projection * projection, axis=0, keepdims=True)

    energy = lax.fori_loop(0, block // tile, some, jnp.zeros((1, 2 * group), f32))
    high = energy.astype(bf16).astype(f32)
    middle = (energy - high).astype(bf16).astype(f32)
    parts = [high, middle, energy - high - middle, jnp.zeros((13, 2 * group), f32)]
    parts = jnp.concatenate(parts)
    out_ref[block:] = parts.astype(bf16)


def project(order, pieces, planes, classes, own_o, depth):
    block = pieces[0].shape[1]
    group = classes * own_o
    vmem = pl.BlockSpec(memory_space=pltpu.VMEM)
    return pl.pallas_call(
        lambda *refs: project_kernel(planes, classes, own_o, depth, *refs),
        in_specs=[pl.BlockSpec(memory_space=pltpu.SMEM)] + [vmem] * len(pieces),
        out_specs=[vmem] * 3,
        out_shape=[
            jax.ShapeDtypeStruct((block + 16, 2 * group), bf16),
            jax.ShapeDtypeStruct((1, 2 * group), f32),
            jax.ShapeDtypeStruct((2 * len(pieces), depth, group), f32),
        ],
        compiler_params=params,
        cost_estimate=cost(8 * len(pieces) * planes * classes * group * block, *pieces),
        name="project",
    )(order, *pieces)


def match_kernel(order_ref, mine_ref, theirs_ref, *refs):
    pieces, out_ref, pixels_ref = refs[:-2], refs[-2], refs[-1]
    half = mine_ref.shape[0] - 16
    core = order_ref[0] & 1
    exact = pieces[0].shape[0] % 16 == 0
    stack = [piece[...] if exact else piece[...].astype(f32) for piece in pieces]
    pixels_ref[...] = jnp.concatenate(stack).astype(bf16)
    squares = mine_ref[half:].astype(f32) + theirs_ref[half:].astype(f32)
    energy = jnp.sum(squares, axis=0, keepdims=True)
    total = -0.5 * energy
    for side, projection in ((core, mine_ref), (1 - core, theirs_ref)):
        columns = pl.ds(pl.multiple_of(side * half, half), half)
        total += jnp.dot(pixels_ref[:, columns], projection[:half], preferred_element_type=f32)
    out_ref[...] = total.reshape(out_ref.shape)


def match(order, mine, theirs, batches):
    pieces = sum(batches, [])
    rows, block = pieces[0].shape
    rows_all = rows * len(pieces)
    columns = mine.shape[1]
    vmem = pl.BlockSpec(memory_space=pltpu.VMEM)
    return pl.pallas_call(
        match_kernel,
        in_specs=[pl.BlockSpec(memory_space=pltpu.SMEM)] + [vmem] * (2 + len(pieces)),
        out_specs=[vmem] * 2,
        out_shape=[
            jax.ShapeDtypeStruct((len(batches), rows_all // len(batches), columns), f32),
            jax.ShapeDtypeStruct((rows_all, block), bf16),
        ],
        compiler_params=params,
        cost_estimate=cost(2 * rows_all * block * columns, mine, theirs, *pieces),
        name="match",
    )(order, mine, theirs, *pieces)


def pick(blocks, order):
    return jnp.concatenate([lax.dynamic_slice_in_dim(blocks, i, 1) for i in order])


def in_three(value):
    high = lax.reduce_precision(value, 8, 7)
    rest = value - high
    middle = lax.reduce_precision(rest, 8, 7)
    return [part.astype(bf16) for part in (high, middle, rest - middle)]


def local(volumes, band_weights, band_start, images, noise_precision, log_prior):
    planes, classes, block = volumes.shape
    slabs, batches = lax.axis_size("slab"), lax.axis_size("batch")
    slab, batch = lax.axis_index("slab"), lax.axis_index("batch")
    core = slab & 1
    chips = slabs // 2
    own_o, taps = band_weights.shape[1:]
    particles = images.shape[0]
    rows = particles // slabs
    width = planes * classes
    group = classes * own_o
    own_order, other_order = block_orders()

    def part_for(step):
        column = lax.rem(batch + step, batches) * block
        return lax.dynamic_slice(images, (slab * rows, column), (rows, block))

    half = batches // 2
    steps = [step for step in range(1, batches) if step != half]
    steps = steps + [half]
    parts = [part_for(step) for step in steps]
    fetched = [shifted(part, "batch", step) for part, step in zip(parts, steps)]

    coarse = band_start // 128
    table = jnp.concatenate(
        [
            band_weights.reshape(group, taps).T,
            jnp.stack([coarse, band_start - 128 * coarse]).reshape(2, group).astype(bf16),
            jnp.stack(in_three(log_prior)).reshape(3, group),
        ]
    )
    depth = table.shape[0]
    side = block // 2
    extra = -(-table.size // side)
    table = jnp.pad(table.reshape(-1), (0, extra * side - table.size)).reshape(extra, side)
    flat = after(volumes, *parts).reshape(width, block)
    mine = lax.dynamic_slice_in_dim(flat, core * side, side, axis=1)
    give = lax.dynamic_slice_in_dim(flat, (1 - core) * side, side, axis=1)
    theirs = paired(jnp.concatenate([give, table]), (1, 1))
    shard = jnp.concatenate([mine, theirs[:width], table, theirs[width:]])
    shards = spread_start(shard)
    if len(shards) > 1:
        shards[1] = after(shards[1], *fetched[:1])
    shards = spread_end(shards)
    near = []
    for part in fetched[:-1]:
        ties = (near[-1]) if near else (shards[1:])
        near.append(spread_start(after(part, *ties)))
    order = jnp.stack(own_order)
    mine, prior, tables = project(order, shards, planes, classes, own_o, depth)
    held = []
    mine = after(mine, fetched[-1], *sum(near, []))
    theirs = paired(mine, (1, 1))

    own = [lax.dynamic_slice(images, (i * rows, batch * block), (rows, block)) for i in own_order]
    total, pixels = match(order, mine, theirs, [own])
    total = total[0]
    pixels = [pixels]
    last = spread_start(fetched[-1])
    for step, each in zip(steps, near):
        part, pixel = match(order, mine, theirs, [spread_end(each)])
        pixels.append(pixel)
        total = total + shifted(part[0], "batch", -step)
    part, pixel = match(order, mine, theirs, [spread_end(last)])
    pixels.append(pixel)
    total = total + shifted(part[0], "batch", -steps[-1])
    total = total.reshape(chips, rows, 2 * group)

    def by_rows(blocks):
        return pick(blocks, chip_places(core))

    noise = lax.dynamic_index_in_dim(noise_precision.reshape(chips, 2, rows), core, 1, False)
    score = noise[:, :, None] * by_rows(total) + prior
    own_top = jnp.max(score, axis=2)
    shifted_exp = jnp.exp(score - own_top[:, :, None])
    own_total = jnp.sum(shifted_exp, axis=2)
    count = chips * rows
    lines = -(-count // (2 * group))
    sides = jnp.stack(in_three(own_top.reshape(count)) + in_three(own_total.reshape(count)))
    sides = jnp.pad(sides, ((0, 0), (0, lines * 2 * group - count))).reshape(-1, 2 * group)
    packed = jnp.concatenate([shifted_exp.astype(bf16).reshape(count, 2 * group), sides])
    packed = [packed] + [paired(packed, (2 * i, 2 * i)) for i in range(1, chips)]
    packed = jnp.stack(packed)
    exps = packed[:, :count]
    sides = packed[:, count:].reshape(chips, 6, lines * 2 * group)[:, :, :count].astype(f32)
    tops = sides[:, 0] + sides[:, 1] + sides[:, 2]
    totals = sides[:, 3] + sides[:, 4] + sides[:, 5]
    top = jnp.max(tops, axis=0)
    log_evidence = top + jnp.log(jnp.sum(totals * jnp.exp(tops - top), axis=0))
    scale = jnp.exp(tops - log_evidence)
    weights = (exps.astype(f32) * scale[:, :, None]).astype(bf16)

    chip_order = [i // 2 for i in own_order]
    places = list(zip(held_masks(slabs, 0), held_masks(slabs, 1)))
    places = [(even + core * (odd - even)) // 2 for even, odd in places]
    both = pick(window_slices(order, tables, planes, classes, own_o), places)
    inserted = jnp.einsum("qzo,qno->nz", both, weights, preferred_element_type=f32).astype(bf16)
    inserted = pick(inserted.reshape(chips, rows, 2 * width), chip_order)
    inserted = inserted.reshape(count, 2 * width)
    there = [inserted] + [shifted(inserted, "batch", step) for step in steps]

    responsibilities = jnp.exp(score.reshape(count, 2 * group) - log_evidence[:, None])
    lines = -(-count // group)
    evidence = jnp.pad(log_evidence, (0, lines * group - count)).reshape(lines, group)
    halves = even_first(responsibilities[:, :group], responsibilities[:, group:], core)
    mine = jnp.concatenate([halves[0], evidence])
    theirs = paired(jnp.concatenate([halves[1], evidence]), (1, 1))

    def in_order(one, two):
        return jnp.stack(even_first(one, two, core), axis=1)

    responsibilities = in_order(
        mine[:count].reshape(chips, rows, group), theirs[:count].reshape(chips, rows, group)
    ).reshape(particles, group)
    evidence = [each[count:].reshape(-1)[:count].reshape(chips, rows) for each in (mine, theirs)]
    log_evidence = in_order(*evidence).reshape(particles)

    there[0] = after(there[0], theirs)
    keep, give = sum_images(there, pixels)
    backprojection = add_parts(keep, paired(give, (1, 1)), classes)
    return (
        responsibilities.T.reshape(classes, own_o, particles),
        log_evidence,
        backprojection,
    )


def solution(mesh):
    in_specs = (
        P("slab", None, "batch"),
        P(None, "slab", None),
        P(None, "slab"),
        P("batch", None),
        P("batch"),
        P(None, "slab"),
    )
    out_specs = (P(None, "slab", "batch"), P("batch"), P("slab", None, "batch"))
    return jax.shard_map(local, mesh=mesh, in_specs=in_specs, out_specs=out_specs, check_vma=False)
```

```python
import jax
import jax.numpy as jnp
from jax import lax
from jax.experimental import pallas as pl
from jax.experimental.pallas import tpu as pltpu
from jax.sharding import PartitionSpec as P

f32, bf16 = jnp.float32, jnp.bfloat16
params = pltpu.CompilerParams(vmem_limit_bytes=60 << 20)


def cost(flops, *arrays):
    size = sum(array.size * array.dtype.itemsize for array in arrays)
    return pl.CostEstimate(flops=flops, bytes_accessed=size, transcendentals=0)


def after(value, *others):
    return lax.optimization_barrier((value,) + others)[0]


def turned_taps(table, classes, own_o):
    depth, group = table.shape
    taps = depth - 5
    period = taps * classes
    tap = lax.broadcasted_iota(jnp.int32, (period, taps), 1)
    row = lax.broadcasted_iota(jnp.int32, (period, taps), 0)
    spread = jnp.where(row // classes == tap, 1.0, 0.0).astype(bf16)
    base = jnp.dot(spread, table[:taps].astype(bf16), preferred_element_type=f32)
    start = 128.0 * table[taps : taps + 1] + table[taps + 1 : taps + 2]
    start = start.astype(jnp.int32)
    for bit in range((taps - 1).bit_length()):
        moved = pltpu.roll(base, classes << bit, 0)
        base = jnp.where(start & (1 << bit) != 0, moved, base)
    row = lax.broadcasted_iota(jnp.int32, (period, group), 0)
    column = lax.broadcasted_iota(jnp.int32, (period, group), 1)
    return jnp.where(row % classes == column // own_o, base, 0.0), start


def window(turned, slab, planes, taps, classes):
    base, start = turned
    if planes % taps == 0:
        rows = jnp.concatenate([base] * (planes // taps))
    else:
        width = planes * classes
        rows = base[:width]
        for i in range(1, taps // planes):
            rows = jnp.where(
                slab % (taps // planes) == i, base[i * width : (i + 1) * width], rows
            )
    row = lax.broadcasted_iota(jnp.int32, rows.shape, 0)
    place = slab * planes + row // classes - start
    return jnp.where(jnp.logical_and(place >= 0, place < taps), rows, 0.0)


def even_first(one, two, core):
    return [jnp.where(core == 0, one, two), jnp.where(core == 0, two, one)]


def window_kernel(planes, classes, own_o, order_ref, tables_ref, out_ref):
    group = tables_ref.shape[2]
    taps = tables_ref.shape[1] - 5
    width = planes * classes
    core = order_ref[0] & 1
    for i in range(out_ref.shape[0]):
        tables = even_first(tables_ref[2 * i], tables_ref[2 * i + 1], core)
        for side, table in enumerate(tables):
            turned = turned_taps(table, classes, own_o)
            for part, slab in enumerate((order_ref[0], order_ref[0] ^ 1)):
                rows = window(turned, slab, planes, taps, classes)
                out_ref[
                    i, part * width : (part + 1) * width, side * group : (side + 1) * group
                ] = rows.astype(bf16)


def window_slices(order, tables, planes, classes, own_o):
    slabs, _, group = tables.shape
    vmem = pl.BlockSpec(memory_space=pltpu.VMEM)
    return pl.pallas_call(
        lambda *refs: window_kernel(planes, classes, own_o, *refs),
        in_specs=[pl.BlockSpec(memory_space=pltpu.SMEM), vmem],
        out_specs=vmem,
        out_shape=jax.ShapeDtypeStruct((slabs // 2, 2 * planes * classes, 2 * group), bf16),
        compiler_params=params,
        cost_estimate=cost(0, tables),
        name="window_slices",
    )(order, tables)


def shifted(value, axis, step):
    size = lax.axis_size(axis)
    return lax.ppermute(value, axis, [(i, (i + step) % size) for i in range(size)])


def paired(value, masks):
    size = lax.axis_size("slab")
    return lax.ppermute(value, "slab", [(i, i ^ masks[i % 2]) for i in range(size)])


def mask_steps(size):
    bits = [1 << i for i in range(1, size.bit_length() - 1)]
    return list(zip(bits, reversed(bits)))


def held_masks(size, core):
    masks = [0]
    for step in mask_steps(size):
        masks = masks + [mask ^ step[core] for mask in masks]
    return masks


def block_orders():
    size = lax.axis_size("slab")
    slab = lax.axis_index("slab")
    core = slab & 1
    masks = list(zip(held_masks(size, 0), held_masks(size, 1)))
    own = [slab ^ (even + core * (odd - even)) for even, odd in masks]
    other = [slab ^ 1 ^ (odd + core * (even - odd)) for even, odd in masks]
    return own, other


def chip_places(parity):
    chips = lax.axis_size("slab") // 2
    chip = lax.axis_index("slab") // 2
    depth = chips.bit_length() - 1
    places = []
    for other in range(chips):
        apart = chip ^ other
        turned = sum(((apart >> i) & 1) << (depth - 1 - i) for i in range(depth))
        places.append(apart + parity * (turned - apart))
    return places


def spread_start(block):
    return [block] + [paired(block, step) for step in mask_steps(lax.axis_size("slab"))]


def spread_end(blocks):
    held = blocks[:2]
    for step, block in zip(mask_steps(lax.axis_size("slab"))[1:], blocks[2:]):
        held = held + [block] + [paired(each, step) for each in held[1:]]
    return held


def sum_images_kernel(*refs):
    count = refs[-1].shape[0]
    values = [ref for ref in refs[:-2] if ref.shape[1] == 2 * count]
    pixels = refs[len(values) : -2]
    rows = values[0].shape[0]
    contract = (((0,), (0,)), ((), ()))
    total = 0.0
    place = 0
    for pixel in pixels:
        for top in range(0, pixel.shape[0], rows):
            total += lax.dot_general(
                values[place][...],
                pixel[top : top + rows],
                contract,
                preferred_element_type=f32,
            )
            place += 1
    refs[-2][...] = total[:count]
    refs[-1][...] = total[count:].astype(bf16)


def sum_images(values, pixels):
    rows, width = values[0].shape
    block = pixels[0].shape[1]
    tile = min(block, 2048)
    half = jax.ShapeDtypeStruct((width // 2, block), f32)
    return pl.pallas_call(
        sum_images_kernel,
        grid=(block // tile,),
        in_specs=[pl.BlockSpec((rows, width), lambda i: (0, 0))] * len(values)
        + [pl.BlockSpec((pixel.shape[0], tile), lambda i: (0, i)) for pixel in pixels],
        out_specs=[pl.BlockSpec((width // 2, tile), lambda i: (0, i))] * 2,
        out_shape=[half, jax.ShapeDtypeStruct((width // 2, block), bf16)],
        compiler_params=params,
        cost_estimate=cost(2 * rows * len(values) * width * block, *values, *pixels),
        name="sum_images",
    )(*values, *pixels)


def add_parts_kernel(one_ref, two_ref, out_ref):
    total = one_ref[...] + two_ref[...]
    out_ref[...] = total.reshape(out_ref.shape)


def add_parts(one, two, classes):
    width, block = one.shape
    tile = min(block, 4096)
    part = pl.BlockSpec((width, tile), lambda i: (0, i))
    return pl.pallas_call(
        add_parts_kernel,
        grid=(block // tile,),
        in_specs=[part] * 2,
        out_specs=pl.BlockSpec((width // classes, classes, tile), lambda i: (0, 0, i)),
        out_shape=jax.ShapeDtypeStruct((width // classes, classes, block), f32),
        compiler_params=params,
        cost_estimate=cost(2 * width * block, one, two, one),
        name="add_parts",
    )(one, two)


def project_kernel(planes, classes, own_o, depth, order_ref, *refs):
    pieces, (out_ref, prior_ref, tables_ref) = refs[:-3], refs[-3:]
    width = planes * classes
    group = classes * own_o
    taps = depth - 5
    block = pieces[0].shape[1]
    core = order_ref[0] & 1
    lines = -(-depth * group // block)
    for i, piece in enumerate(pieces):
        flat = piece[2 * width :].astype(f32)
        for side in range(2):
            table = []
            for line in range(depth):
                row, column = divmod(line * group, block)
                row += side * lines
                table.append(flat[row : row + 1, column : column + group])
            tables_ref[2 * i + side] = jnp.concatenate(table)
    chip = even_first(tables_ref[0], tables_ref[1], core)
    prior = [jnp.sum(table[taps + 2 :], axis=0, keepdims=True) for table in chip]
    prior_ref[...] = jnp.concatenate(prior, axis=1)
    turned = [turned_taps(table, classes, own_o) for table in chip]
    slices = []
    for i in range(len(pieces)):
        for slab in (order_ref[i], order_ref[i] ^ 1):
            parts = [window(one, slab, planes, taps, classes) for one in turned]
            slices.append(jnp.concatenate(parts, axis=1))
    slices = jnp.concatenate(slices).T.astype(bf16)
    tile = min(block, 512)

    def some(i, energy):
        columns = pl.ds(pl.multiple_of(i * tile, tile), tile)
        stack = jnp.concatenate([piece[: 2 * width, columns] for piece in pieces])
        projection = jnp.dot(slices, stack, preferred_element_type=f32)
        projection = projection.astype(bf16).astype(f32).T
        out_ref[columns] = projection.astype(bf16)
        return energy + jnp.sum(projection * projection, axis=0, keepdims=True)

    energy = lax.fori_loop(0, block // tile, some, jnp.zeros((1, 2 * group), f32))
    high = energy.astype(bf16).astype(f32)
    middle = (energy - high).astype(bf16).astype(f32)
    parts = [high, middle, energy - high - middle, jnp.zeros((13, 2 * group), f32)]
    parts = jnp.concatenate(parts)
    out_ref[block:] = parts.astype(bf16)


def project(order, pieces, planes, classes, own_o, depth):
    block = pieces[0].shape[1]
    group = classes * own_o
    vmem = pl.BlockSpec(memory_space=pltpu.VMEM)
    return pl.pallas_call(
        lambda *refs: project_kernel(planes, classes, own_o, depth, *refs),
        in_specs=[pl.BlockSpec(memory_space=pltpu.SMEM)] + [vmem] * len(pieces),
        out_specs=[vmem] * 3,
        out_shape=[
            jax.ShapeDtypeStruct((block + 16, 2 * group), bf16),
            jax.ShapeDtypeStruct((1, 2 * group), f32),
            jax.ShapeDtypeStruct((2 * len(pieces), depth, group), f32),
        ],
        compiler_params=params,
        cost_estimate=cost(8 * len(pieces) * planes * classes * group * block, *pieces),
        name="project",
    )(order, *pieces)


def match_kernel(order_ref, mine_ref, theirs_ref, *refs):
    pieces, out_ref, pixels_ref = refs[:-2], refs[-2], refs[-1]
    half = mine_ref.shape[0] - 16
    core = order_ref[0] & 1
    exact = pieces[0].shape[0] % 16 == 0
    stack = [piece[...] if exact else piece[...].astype(f32) for piece in pieces]
    pixels_ref[...] = jnp.concatenate(stack).astype(bf16)
    squares = mine_ref[half:].astype(f32) + theirs_ref[half:].astype(f32)
    energy = jnp.sum(squares, axis=0, keepdims=True)
    total = -0.5 * energy
    for side, projection in ((core, mine_ref), (1 - core, theirs_ref)):
        columns = pl.ds(pl.multiple_of(side * half, half), half)
        total += jnp.dot(pixels_ref[:, columns], projection[:half], preferred_element_type=f32)
    out_ref[...] = total.reshape(out_ref.shape)


def match(order, mine, theirs, batches):
    pieces = sum(batches, [])
    rows, block = pieces[0].shape
    rows_all = rows * len(pieces)
    columns = mine.shape[1]
    vmem = pl.BlockSpec(memory_space=pltpu.VMEM)
    return pl.pallas_call(
        match_kernel,
        in_specs=[pl.BlockSpec(memory_space=pltpu.SMEM)] + [vmem] * (2 + len(pieces)),
        out_specs=[vmem] * 2,
        out_shape=[
            jax.ShapeDtypeStruct((len(batches), rows_all // len(batches), columns), f32),
            jax.ShapeDtypeStruct((rows_all, block), bf16),
        ],
        compiler_params=params,
        cost_estimate=cost(2 * rows_all * block * columns, mine, theirs, *pieces),
        name="match",
    )(order, mine, theirs, *pieces)


def pick(blocks, order):
    return jnp.concatenate([lax.dynamic_slice_in_dim(blocks, i, 1) for i in order])


def in_three(value):
    high = lax.reduce_precision(value, 8, 7)
    rest = value - high
    middle = lax.reduce_precision(rest, 8, 7)
    return [part.astype(bf16) for part in (high, middle, rest - middle)]


def local(volumes, band_weights, band_start, images, noise_precision, log_prior):
    planes, classes, block = volumes.shape
    slabs, batches = lax.axis_size("slab"), lax.axis_size("batch")
    slab, batch = lax.axis_index("slab"), lax.axis_index("batch")
    core = slab & 1
    chips = slabs // 2
    own_o, taps = band_weights.shape[1:]
    particles = images.shape[0]
    rows = particles // slabs
    width = planes * classes
    group = classes * own_o
    own_order, other_order = block_orders()

    def part_for(step):
        column = lax.rem(batch + step, batches) * block
        return lax.dynamic_slice(images, (slab * rows, column), (rows, block))

    half = batches // 2
    steps = [step for step in range(1, batches) if step != half]
    steps = steps + [half]
    parts = [part_for(step) for step in steps]
    fetched = [shifted(part, "batch", step) for part, step in zip(parts, steps)]

    coarse = band_start // 128
    table = jnp.concatenate(
        [
            band_weights.reshape(group, taps).T,
            jnp.stack([coarse, band_start - 128 * coarse]).reshape(2, group).astype(bf16),
            jnp.stack(in_three(log_prior)).reshape(3, group),
        ]
    )
    depth = table.shape[0]
    side = block // 2
    extra = -(-table.size // side)
    table = jnp.pad(table.reshape(-1), (0, extra * side - table.size)).reshape(extra, side)
    flat = after(volumes, *parts).reshape(width, block)
    mine = lax.dynamic_slice_in_dim(flat, core * side, side, axis=1)
    give = lax.dynamic_slice_in_dim(flat, (1 - core) * side, side, axis=1)
    theirs = paired(jnp.concatenate([give, table]), (1, 1))
    shard = jnp.concatenate([mine, theirs[:width], table, theirs[width:]])
    shards = spread_start(shard)
    if len(shards) > 1:
        shards[1] = after(shards[1], *fetched[:1])
    shards = spread_end(shards)
    near = []
    for part in fetched[:-1]:
        ties = (near[-1]) if near else (shards[1:])
        near.append(spread_start(after(part, *ties)))
    order = jnp.stack(own_order)
    mine, prior, tables = project(order, shards, planes, classes, own_o, depth)
    held = []
    mine = after(mine, fetched[-1], *sum(near, []))
    theirs = paired(mine, (1, 1))

    later = after(images, mine)
    own = [lax.dynamic_slice(later, (i * rows, batch * block), (rows, block)) for i in own_order]
    total, pixels = match(order, mine, theirs, [own])
    total = total[0]
    pixels = [pixels]
    last = spread_start(fetched[-1])
    for step, each in zip(steps, near):
        part, pixel = match(order, mine, theirs, [spread_end(each)])
        pixels.append(pixel)
        total = total + shifted(part[0], "batch", -step)
    part, pixel = match(order, mine, theirs, [spread_end(last)])
    pixels.append(pixel)
    total = total + shifted(part[0], "batch", -steps[-1])
    total = total.reshape(chips, rows, 2 * group)

    def by_rows(blocks):
        return pick(blocks, chip_places(core))

    noise, prior = lax.optimization_barrier((noise_precision, prior, part))[:2]
    noise = lax.dynamic_index_in_dim(noise.reshape(chips, 2, rows), core, 1, False)
    score = noise[:, :, None] * by_rows(total) + prior
    own_top = jnp.max(score, axis=2)
    shifted_exp = jnp.exp(score - own_top[:, :, None])
    own_total = jnp.sum(shifted_exp, axis=2)
    count = chips * rows
    lines = -(-count // (2 * group))
    sides = jnp.stack(in_three(own_top.reshape(count)) + in_three(own_total.reshape(count)))
    sides = jnp.pad(sides, ((0, 0), (0, lines * 2 * group - count))).reshape(-1, 2 * group)
    packed = jnp.concatenate([shifted_exp.astype(bf16).reshape(count, 2 * group), sides])
    packed = [packed] + [paired(packed, (2 * i, 2 * i)) for i in range(1, chips)]
    packed = jnp.stack(packed)
    exps = packed[:, :count]
    sides = packed[:, count:].reshape(chips, 6, lines * 2 * group)[:, :, :count].astype(f32)
    tops = sides[:, 0] + sides[:, 1] + sides[:, 2]
    totals = sides[:, 3] + sides[:, 4] + sides[:, 5]
    top = jnp.max(tops, axis=0)
    log_evidence = top + jnp.log(jnp.sum(totals * jnp.exp(tops - top), axis=0))
    scale = jnp.exp(tops - log_evidence)
    weights = (exps.astype(f32) * scale[:, :, None]).astype(bf16)

    chip_order = [i // 2 for i in own_order]
    places = list(zip(held_masks(slabs, 0), held_masks(slabs, 1)))
    places = [(even + core * (odd - even)) // 2 for even, odd in places]
    both = pick(window_slices(order, after(tables, part), planes, classes, own_o), places)
    inserted = jnp.einsum("qzo,qno->nz", both, weights, preferred_element_type=f32).astype(bf16)
    inserted = pick(inserted.reshape(chips, rows, 2 * width), chip_order)
    inserted = inserted.reshape(count, 2 * width)
    there = [inserted] + [shifted(inserted, "batch", step) for step in steps]

    responsibilities = jnp.exp(score.reshape(count, 2 * group) - log_evidence[:, None])
    lines = -(-count // group)
    evidence = jnp.pad(log_evidence, (0, lines * group - count)).reshape(lines, group)
    halves = even_first(responsibilities[:, :group], responsibilities[:, group:], core)
    mine = jnp.concatenate([halves[0], evidence])
    theirs = paired(jnp.concatenate([halves[1], evidence]), (1, 1))

    def in_order(one, two):
        return jnp.stack(even_first(one, two, core), axis=1)

    responsibilities = in_order(
        mine[:count].reshape(chips, rows, group), theirs[:count].reshape(chips, rows, group)
    ).reshape(particles, group)
    evidence = [each[count:].reshape(-1)[:count].reshape(chips, rows) for each in (mine, theirs)]
    log_evidence = in_order(*evidence).reshape(particles)

    there[0] = after(there[0], theirs)
    keep, give = sum_images(there, pixels)
    backprojection = add_parts(keep, paired(give, (1, 1)), classes)
    return (
        responsibilities.T.reshape(classes, own_o, particles),
        log_evidence,
        backprojection,
    )


def solution(mesh):
    in_specs = (
        P("slab", None, "batch"),
        P(None, "slab", None),
        P(None, "slab"),
        P("batch", None),
        P("batch"),
        P(None, "slab"),
    )
    out_specs = (P(None, "slab", "batch"), P("batch"), P("slab", None, "batch"))
    return jax.shard_map(local, mesh=mesh, in_specs=in_specs, out_specs=out_specs, check_vma=False)
```

```python
import jax
import jax.numpy as jnp
from jax import lax
from jax.experimental import pallas as pl
from jax.experimental.pallas import tpu as pltpu
from jax.sharding import PartitionSpec as P

f32, bf16 = jnp.float32, jnp.bfloat16
params = pltpu.CompilerParams(vmem_limit_bytes=66000000)


def cost(flops, *arrays):
    size = sum(array.size * array.dtype.itemsize for array in arrays)
    return pl.CostEstimate(flops=flops, bytes_accessed=size, transcendentals=0)


def after(value, *others):
    return lax.optimization_barrier((value,) + others)[0]


def turned_taps(table, classes, own_o):
    depth, group = table.shape
    taps = depth - 5
    period = taps * classes
    tap = lax.broadcasted_iota(jnp.int32, (period, taps), 1)
    row = lax.broadcasted_iota(jnp.int32, (period, taps), 0)
    spread = jnp.where(row // classes == tap, 1.0, 0.0).astype(bf16)
    base = jnp.dot(spread, table[:taps].astype(bf16), preferred_element_type=f32)
    start = 128.0 * table[taps : taps + 1] + table[taps + 1 : taps + 2]
    start = start.astype(jnp.int32)
    for bit in range((taps - 1).bit_length()):
        moved = pltpu.roll(base, classes << bit, 0)
        base = jnp.where(start & (1 << bit) != 0, moved, base)
    row = lax.broadcasted_iota(jnp.int32, (period, group), 0)
    column = lax.broadcasted_iota(jnp.int32, (period, group), 1)
    return jnp.where(row % classes == column // own_o, base, 0.0), start


def window(turned, slab, planes, taps, classes):
    base, start = turned
    if planes % taps == 0:
        rows = jnp.concatenate([base] * (planes // taps))
    else:
        width = planes * classes
        rows = base[:width]
        for i in range(1, taps // planes):
            rows = jnp.where(
                slab % (taps // planes) == i, base[i * width : (i + 1) * width], rows
            )
    row = lax.broadcasted_iota(jnp.int32, rows.shape, 0)
    place = slab * planes + row // classes - start
    return jnp.where(jnp.logical_and(place >= 0, place < taps), rows, 0.0)


def even_first(one, two, core):
    return [jnp.where(core == 0, one, two), jnp.where(core == 0, two, one)]


def window_kernel(planes, classes, own_o, order_ref, tables_ref, out_ref):
    group = tables_ref.shape[2]
    taps = tables_ref.shape[1] - 5
    width = planes * classes
    core = order_ref[0] & 1
    for i in range(out_ref.shape[0]):
        tables = even_first(tables_ref[2 * i], tables_ref[2 * i + 1], core)
        for side, table in enumerate(tables):
            turned = turned_taps(table, classes, own_o)
            for part, slab in enumerate((order_ref[0], order_ref[0] ^ 1)):
                rows = window(turned, slab, planes, taps, classes)
                out_ref[
                    i, part * width : (part + 1) * width, side * group : (side + 1) * group
                ] = rows.astype(bf16)


def window_slices(order, tables, planes, classes, own_o):
    slabs, _, group = tables.shape
    vmem = pl.BlockSpec(memory_space=pltpu.VMEM)
    return pl.pallas_call(
        lambda *refs: window_kernel(planes, classes, own_o, *refs),
        in_specs=[pl.BlockSpec(memory_space=pltpu.SMEM), vmem],
        out_specs=vmem,
        out_shape=jax.ShapeDtypeStruct((slabs // 2, 2 * planes * classes, 2 * group), bf16),
        compiler_params=params,
        cost_estimate=cost(0, tables),
        name="window_slices",
    )(order, tables)


def shifted(value, axis, step):
    size = lax.axis_size(axis)
    return lax.ppermute(value, axis, [(i, (i + step) % size) for i in range(size)])


def paired(value, masks):
    size = lax.axis_size("slab")
    return lax.ppermute(value, "slab", [(i, i ^ masks[i % 2]) for i in range(size)])


def mask_steps(size):
    bits = [1 << i for i in range(1, size.bit_length() - 1)]
    return list(zip(bits, reversed(bits)))


def held_masks(size, core):
    masks = [0]
    for step in mask_steps(size):
        masks = masks + [mask ^ step[core] for mask in masks]
    return masks


def block_orders():
    size = lax.axis_size("slab")
    slab = lax.axis_index("slab")
    core = slab & 1
    masks = list(zip(held_masks(size, 0), held_masks(size, 1)))
    own = [slab ^ (even + core * (odd - even)) for even, odd in masks]
    other = [slab ^ 1 ^ (odd + core * (even - odd)) for even, odd in masks]
    return own, other


def chip_places(parity):
    chips = lax.axis_size("slab") // 2
    chip = lax.axis_index("slab") // 2
    depth = chips.bit_length() - 1
    places = []
    for other in range(chips):
        apart = chip ^ other
        turned = sum(((apart >> i) & 1) << (depth - 1 - i) for i in range(depth))
        places.append(apart + parity * (turned - apart))
    return places


def spread_start(block):
    return [block] + [paired(block, step) for step in mask_steps(lax.axis_size("slab"))]


def spread_end(blocks):
    held = blocks[:2]
    for step, block in zip(mask_steps(lax.axis_size("slab"))[1:], blocks[2:]):
        held = held + [block] + [paired(each, step) for each in held[1:]]
    return held


def sum_images_kernel(*refs):
    count = refs[-1].shape[0]
    values = [ref for ref in refs[:-2] if ref.shape[1] == 2 * count]
    pixels = refs[len(values) : -2]
    rows = values[0].shape[0]
    contract = (((0,), (0,)), ((), ()))
    total = 0.0
    place = 0
    for pixel in pixels:
        for top in range(0, pixel.shape[0], rows):
            total += lax.dot_general(
                values[place][...],
                pixel[top : top + rows],
                contract,
                preferred_element_type=f32,
            )
            place += 1
    refs[-2][...] = total[:count]
    refs[-1][...] = total[count:].astype(bf16)


def sum_images(values, pixels):
    rows, width = values[0].shape
    block = pixels[0].shape[1]
    tile = min(block, 2048)
    half = jax.ShapeDtypeStruct((width // 2, block), f32)
    return pl.pallas_call(
        sum_images_kernel,
        grid=(block // tile,),
        in_specs=[pl.BlockSpec((rows, width), lambda i: (0, 0))] * len(values)
        + [pl.BlockSpec((pixel.shape[0], tile), lambda i: (0, i)) for pixel in pixels],
        out_specs=[pl.BlockSpec((width // 2, tile), lambda i: (0, i))] * 2,
        out_shape=[half, jax.ShapeDtypeStruct((width // 2, block), bf16)],
        compiler_params=params,
        cost_estimate=cost(2 * rows * len(values) * width * block, *values, *pixels),
        name="sum_images",
    )(*values, *pixels)


def add_parts_kernel(one_ref, two_ref, out_ref):
    total = one_ref[...] + two_ref[...]
    out_ref[...] = total.reshape(out_ref.shape)


def add_parts(one, two, classes):
    width, block = one.shape
    tile = min(block, 2048)
    part = pl.BlockSpec((width, tile), lambda i: (0, i))
    return pl.pallas_call(
        add_parts_kernel,
        grid=(block // tile,),
        in_specs=[part] * 2,
        out_specs=pl.BlockSpec((width // classes, classes, tile), lambda i: (0, 0, i)),
        out_shape=jax.ShapeDtypeStruct((width // classes, classes, block), f32),
        compiler_params=params,
        cost_estimate=cost(2 * width * block, one, two, one),
        name="add_parts",
    )(one, two)


def project_kernel(planes, classes, own_o, depth, order_ref, *refs):
    pieces, (out_ref, prior_ref, tables_ref) = refs[:-3], refs[-3:]
    width = planes * classes
    group = classes * own_o
    taps = depth - 5
    block = pieces[0].shape[1]
    core = order_ref[0] & 1
    lines = -(-depth * group // block)
    for i, piece in enumerate(pieces):
        flat = piece[2 * width :].astype(f32)
        for side in range(2):
            table = []
            for line in range(depth):
                row, column = divmod(line * group, block)
                row += side * lines
                table.append(flat[row : row + 1, column : column + group])
            tables_ref[2 * i + side] = jnp.concatenate(table)
    chip = even_first(tables_ref[0], tables_ref[1], core)
    prior = [jnp.sum(table[taps + 2 :], axis=0, keepdims=True) for table in chip]
    prior_ref[...] = jnp.concatenate(prior, axis=1)
    turned = [turned_taps(table, classes, own_o) for table in chip]
    slices = []
    for i in range(len(pieces)):
        for slab in (order_ref[i], order_ref[i] ^ 1):
            parts = [window(one, slab, planes, taps, classes) for one in turned]
            slices.append(jnp.concatenate(parts, axis=1))
    slices = jnp.concatenate(slices).T.astype(bf16)
    tile = min(block, 512)

    def some(i, energy):
        columns = pl.ds(pl.multiple_of(i * tile, tile), tile)
        stack = jnp.concatenate([piece[: 2 * width, columns] for piece in pieces])
        projection = jnp.dot(slices, stack, preferred_element_type=f32)
        projection = projection.astype(bf16).astype(f32).T
        out_ref[columns] = projection.astype(bf16)
        return energy + jnp.sum(projection * projection, axis=0, keepdims=True)

    energy = lax.fori_loop(0, block // tile, some, jnp.zeros((1, 2 * group), f32))
    high = energy.astype(bf16).astype(f32)
    middle = (energy - high).astype(bf16).astype(f32)
    parts = [high, middle, energy - high - middle, jnp.zeros((13, 2 * group), f32)]
    parts = jnp.concatenate(parts)
    out_ref[block:] = parts.astype(bf16)


def project(order, pieces, planes, classes, own_o, depth):
    block = pieces[0].shape[1]
    group = classes * own_o
    vmem = pl.BlockSpec(memory_space=pltpu.VMEM)
    return pl.pallas_call(
        lambda *refs: project_kernel(planes, classes, own_o, depth, *refs),
        in_specs=[pl.BlockSpec(memory_space=pltpu.SMEM)] + [vmem] * len(pieces),
        out_specs=[vmem] * 3,
        out_shape=[
            jax.ShapeDtypeStruct((block + 16, 2 * group), bf16),
            jax.ShapeDtypeStruct((1, 2 * group), f32),
            jax.ShapeDtypeStruct((2 * len(pieces), depth, group), f32),
        ],
        compiler_params=params,
        cost_estimate=cost(8 * len(pieces) * planes * classes * group * block, *pieces),
        name="project",
    )(order, *pieces)


def match_kernel(order_ref, mine_ref, theirs_ref, *refs):
    pieces, out_ref, pixels_ref = refs[:-2], refs[-2], refs[-1]
    half = mine_ref.shape[0] - 16
    core = order_ref[0] & 1
    exact = pieces[0].shape[0] % 16 == 0
    stack = [piece[...] if exact else piece[...].astype(f32) for piece in pieces]
    pixels_ref[...] = jnp.concatenate(stack).astype(bf16)
    squares = mine_ref[half:].astype(f32) + theirs_ref[half:].astype(f32)
    energy = jnp.sum(squares, axis=0, keepdims=True)
    total = -0.5 * energy
    for side, projection in ((core, mine_ref), (1 - core, theirs_ref)):
        columns = pl.ds(pl.multiple_of(side * half, half), half)
        total += jnp.dot(pixels_ref[:, columns], projection[:half], preferred_element_type=f32)
    out_ref[...] = total.reshape(out_ref.shape)


def match(order, mine, theirs, batches):
    pieces = sum(batches, [])
    rows, block = pieces[0].shape
    rows_all = rows * len(pieces)
    columns = mine.shape[1]
    vmem = pl.BlockSpec(memory_space=pltpu.VMEM)
    return pl.pallas_call(
        match_kernel,
        in_specs=[pl.BlockSpec(memory_space=pltpu.SMEM)] + [vmem] * (2 + len(pieces)),
        out_specs=[vmem] * 2,
        out_shape=[
            jax.ShapeDtypeStruct((len(batches), rows_all // len(batches), columns), f32),
            jax.ShapeDtypeStruct((rows_all, block), bf16),
        ],
        compiler_params=params,
        cost_estimate=cost(2 * rows_all * block * columns, mine, theirs, *pieces),
        name="match",
    )(order, mine, theirs, *pieces)


def pick(blocks, order):
    return jnp.concatenate([lax.dynamic_slice_in_dim(blocks, i, 1) for i in order])


def in_three(value):
    high = lax.reduce_precision(value, 8, 7)
    rest = value - high
    middle = lax.reduce_precision(rest, 8, 7)
    return [part.astype(bf16) for part in (high, middle, rest - middle)]


def local(volumes, band_weights, band_start, images, noise_precision, log_prior):
    planes, classes, block = volumes.shape
    slabs, batches = lax.axis_size("slab"), lax.axis_size("batch")
    slab, batch = lax.axis_index("slab"), lax.axis_index("batch")
    core = slab & 1
    chips = slabs // 2
    own_o, taps = band_weights.shape[1:]
    particles = images.shape[0]
    rows = particles // slabs
    width = planes * classes
    group = classes * own_o
    own_order, other_order = block_orders()

    def part_for(step):
        column = lax.rem(batch + step, batches) * block
        return lax.dynamic_slice(images, (slab * rows, column), (rows, block))

    half = batches // 2
    steps = [step for step in range(1, batches) if step != half]
    steps = steps + [half]
    parts = [part_for(step) for step in steps]
    fetched = [shifted(part, "batch", step) for part, step in zip(parts, steps)]

    coarse = band_start // 128
    table = jnp.concatenate(
        [
            band_weights.reshape(group, taps).T,
            jnp.stack([coarse, band_start - 128 * coarse]).reshape(2, group).astype(bf16),
            jnp.stack(in_three(log_prior)).reshape(3, group),
        ]
    )
    depth = table.shape[0]
    side = block // 2
    extra = -(-table.size // side)
    table = jnp.pad(table.reshape(-1), (0, extra * side - table.size)).reshape(extra, side)
    flat = after(volumes, *parts).reshape(width, block)
    mine = lax.dynamic_slice_in_dim(flat, core * side, side, axis=1)
    give = lax.dynamic_slice_in_dim(flat, (1 - core) * side, side, axis=1)
    theirs = paired(jnp.concatenate([give, table]), (1, 1))
    shard = jnp.concatenate([mine, theirs[:width], table, theirs[width:]])
    shards = spread_start(shard)
    if len(shards) > 1:
        shards[1] = after(shards[1], *fetched[:1])
    shards = spread_end(shards)
    near = []
    for part in fetched[:-1]:
        ties = (near[-1]) if near else (shards[1:])
        near.append(spread_start(after(part, *ties)))
    order = jnp.stack(own_order)
    mine, prior, tables = project(order, shards, planes, classes, own_o, depth)
    held = []
    mine = after(mine, fetched[-1], *sum(near, []))
    theirs = paired(mine, (1, 1))

    later = after(images, mine)
    own = [lax.dynamic_slice(later, (i * rows, batch * block), (rows, block)) for i in own_order]
    total, pixels = match(order, mine, theirs, [own])
    total = total[0]
    pixels = [pixels]
    last = spread_start(fetched[-1])
    for step, each in zip(steps, near):
        part, pixel = match(order, mine, theirs, [spread_end(each)])
        pixels.append(pixel)
        total = total + shifted(part[0], "batch", -step)
    part, pixel = match(order, mine, theirs, [spread_end(last)])
    pixels.append(pixel)
    total = total + shifted(part[0], "batch", -steps[-1])
    total = total.reshape(chips, rows, 2 * group)

    def by_rows(blocks):
        return pick(blocks, chip_places(core))

    noise, prior = lax.optimization_barrier((noise_precision, prior, part))[:2]
    noise = lax.dynamic_index_in_dim(noise.reshape(chips, 2, rows), core, 1, False)
    score = noise[:, :, None] * by_rows(total) + prior
    own_top = jnp.max(score, axis=2)
    shifted_exp = jnp.exp(score - own_top[:, :, None])
    own_total = jnp.sum(shifted_exp, axis=2)
    count = chips * rows
    lines = -(-count // (2 * group))
    sides = jnp.stack(in_three(own_top.reshape(count)) + in_three(own_total.reshape(count)))
    sides = jnp.pad(sides, ((0, 0), (0, lines * 2 * group - count))).reshape(-1, 2 * group)
    packed = jnp.concatenate([shifted_exp.astype(bf16).reshape(count, 2 * group), sides])
    packed = [packed] + [paired(packed, (2 * i, 2 * i)) for i in range(1, chips)]
    packed = jnp.stack(packed)
    exps = packed[:, :count]
    sides = packed[:, count:].reshape(chips, 6, lines * 2 * group)[:, :, :count].astype(f32)
    tops = sides[:, 0] + sides[:, 1] + sides[:, 2]
    totals = sides[:, 3] + sides[:, 4] + sides[:, 5]
    top = jnp.max(tops, axis=0)
    log_evidence = top + jnp.log(jnp.sum(totals * jnp.exp(tops - top), axis=0))
    scale = jnp.exp(tops - log_evidence)
    weights = (exps.astype(f32) * scale[:, :, None]).astype(bf16)

    chip_order = [i // 2 for i in own_order]
    places = list(zip(held_masks(slabs, 0), held_masks(slabs, 1)))
    places = [(even + core * (odd - even)) // 2 for even, odd in places]
    both = pick(window_slices(order, after(tables, part), planes, classes, own_o), places)
    inserted = jnp.einsum("qzo,qno->nz", both, weights, preferred_element_type=f32).astype(bf16)
    inserted = pick(inserted.reshape(chips, rows, 2 * width), chip_order)
    inserted = inserted.reshape(count, 2 * width)
    there = [inserted] + [shifted(inserted, "batch", step) for step in steps]

    responsibilities = jnp.exp(score.reshape(count, 2 * group) - log_evidence[:, None])
    lines = -(-count // group)
    evidence = jnp.pad(log_evidence, (0, lines * group - count)).reshape(lines, group)
    halves = even_first(responsibilities[:, :group], responsibilities[:, group:], core)
    mine = jnp.concatenate([halves[0], evidence])
    theirs = paired(jnp.concatenate([halves[1], evidence]), (1, 1))

    def in_order(one, two):
        return jnp.stack(even_first(one, two, core), axis=1)

    responsibilities = in_order(
        mine[:count].reshape(chips, rows, group), theirs[:count].reshape(chips, rows, group)
    ).reshape(particles, group)
    evidence = [each[count:].reshape(-1)[:count].reshape(chips, rows) for each in (mine, theirs)]
    log_evidence = in_order(*evidence).reshape(particles)

    there[0] = after(there[0], theirs)
    keep, give = sum_images(there, pixels)
    backprojection = add_parts(keep, paired(give, (1, 1)), classes)
    return (
        responsibilities.T.reshape(classes, own_o, particles),
        log_evidence,
        backprojection,
    )


def solution(mesh):
    in_specs = (
        P("slab", None, "batch"),
        P(None, "slab", None),
        P(None, "slab"),
        P("batch", None),
        P("batch"),
        P(None, "slab"),
    )
    out_specs = (P(None, "slab", "batch"), P("batch"), P("slab", None, "batch"))
    return jax.shard_map(local, mesh=mesh, in_specs=in_specs, out_specs=out_specs, check_vma=False)
```

```python
import jax
import jax.numpy as jnp
from jax import lax
from jax.experimental import pallas as pl
from jax.experimental.pallas import tpu as pltpu
from jax.sharding import PartitionSpec as P

f32, bf16 = jnp.float32, jnp.bfloat16
params = pltpu.CompilerParams(vmem_limit_bytes=66000000)


def cost(flops, *arrays):
    size = sum(array.size * array.dtype.itemsize for array in arrays)
    return pl.CostEstimate(flops=flops, bytes_accessed=size, transcendentals=0)


def after(value, *others):
    return lax.optimization_barrier((value,) + others)[0]


def turned_taps(table, classes, own_o):
    depth, group = table.shape
    taps = depth - 5
    period = taps * classes
    tap = lax.broadcasted_iota(jnp.int32, (period, taps), 1)
    row = lax.broadcasted_iota(jnp.int32, (period, taps), 0)
    spread = jnp.where(row // classes == tap, 1.0, 0.0).astype(bf16)
    base = jnp.dot(spread, table[:taps].astype(bf16), preferred_element_type=f32)
    start = 128.0 * table[taps : taps + 1] + table[taps + 1 : taps + 2]
    start = start.astype(jnp.int32)
    for bit in range((taps - 1).bit_length()):
        moved = pltpu.roll(base, classes << bit, 0)
        base = jnp.where(start & (1 << bit) != 0, moved, base)
    row = lax.broadcasted_iota(jnp.int32, (period, group), 0)
    column = lax.broadcasted_iota(jnp.int32, (period, group), 1)
    return jnp.where(row % classes == column // own_o, base, 0.0), start


def window(turned, slab, planes, taps, classes):
    base, start = turned
    if planes % taps == 0:
        rows = jnp.concatenate([base] * (planes // taps))
    else:
        width = planes * classes
        rows = base[:width]
        for i in range(1, taps // planes):
            rows = jnp.where(
                slab % (taps // planes) == i, base[i * width : (i + 1) * width], rows
            )
    row = lax.broadcasted_iota(jnp.int32, rows.shape, 0)
    place = slab * planes + row // classes - start
    return jnp.where(jnp.logical_and(place >= 0, place < taps), rows, 0.0)


def even_first(one, two, core):
    return [jnp.where(core == 0, one, two), jnp.where(core == 0, two, one)]


def window_kernel(planes, classes, own_o, order_ref, tables_ref, out_ref):
    group = tables_ref.shape[2]
    taps = tables_ref.shape[1] - 5
    width = planes * classes
    core = order_ref[0] & 1
    for i in range(out_ref.shape[0]):
        tables = even_first(tables_ref[2 * i], tables_ref[2 * i + 1], core)
        for side, table in enumerate(tables):
            turned = turned_taps(table, classes, own_o)
            for part, slab in enumerate((order_ref[0], order_ref[0] ^ 1)):
                rows = window(turned, slab, planes, taps, classes)
                out_ref[
                    i, part * width : (part + 1) * width, side * group : (side + 1) * group
                ] = rows.astype(bf16)


def window_slices(order, tables, planes, classes, own_o):
    slabs, _, group = tables.shape
    vmem = pl.BlockSpec(memory_space=pltpu.VMEM)
    return pl.pallas_call(
        lambda *refs: window_kernel(planes, classes, own_o, *refs),
        in_specs=[pl.BlockSpec(memory_space=pltpu.SMEM), vmem],
        out_specs=vmem,
        out_shape=jax.ShapeDtypeStruct((slabs // 2, 2 * planes * classes, 2 * group), bf16),
        compiler_params=params,
        cost_estimate=cost(0, tables),
        name="window_slices",
    )(order, tables)


def shifted(value, axis, step):
    size = lax.axis_size(axis)
    return lax.ppermute(value, axis, [(i, (i + step) % size) for i in range(size)])


def paired(value, masks):
    size = lax.axis_size("slab")
    return lax.ppermute(value, "slab", [(i, i ^ masks[i % 2]) for i in range(size)])


def mask_steps(size):
    bits = [1 << i for i in range(1, size.bit_length() - 1)]
    return list(zip(bits, reversed(bits)))


def held_masks(size, core):
    masks = [0]
    for step in mask_steps(size):
        masks = masks + [mask ^ step[core] for mask in masks]
    return masks


def block_orders():
    size = lax.axis_size("slab")
    slab = lax.axis_index("slab")
    core = slab & 1
    masks = list(zip(held_masks(size, 0), held_masks(size, 1)))
    own = [slab ^ (even + core * (odd - even)) for even, odd in masks]
    other = [slab ^ 1 ^ (odd + core * (even - odd)) for even, odd in masks]
    return own, other


def chip_places(parity):
    chips = lax.axis_size("slab") // 2
    chip = lax.axis_index("slab") // 2
    depth = chips.bit_length() - 1
    places = []
    for other in range(chips):
        apart = chip ^ other
        turned = sum(((apart >> i) & 1) << (depth - 1 - i) for i in range(depth))
        places.append(apart + parity * (turned - apart))
    return places


def spread_start(block):
    return [block] + [paired(block, step) for step in mask_steps(lax.axis_size("slab"))]


def spread_end(blocks):
    held = blocks[:2]
    for step, block in zip(mask_steps(lax.axis_size("slab"))[1:], blocks[2:]):
        held = held + [block] + [paired(each, step) for each in held[1:]]
    return held


def sum_images_kernel(*refs):
    count = refs[-1].shape[0]
    values = [ref for ref in refs[:-2] if ref.shape[1] == 2 * count]
    pixels = refs[len(values) : -2]
    rows = values[0].shape[0]
    contract = (((0,), (0,)), ((), ()))
    total = 0.0
    place = 0
    for pixel in pixels:
        for top in range(0, pixel.shape[0], rows):
            total += lax.dot_general(
                values[place][...],
                pixel[top : top + rows],
                contract,
                preferred_element_type=f32,
            )
            place += 1
    refs[-2][...] = total[:count]
    refs[-1][...] = total[count:].astype(bf16)


def sum_images(values, pixels):
    rows, width = values[0].shape
    block = pixels[0].shape[1]
    tile = min(block, 2048)
    half = jax.ShapeDtypeStruct((width // 2, block), f32)
    return pl.pallas_call(
        sum_images_kernel,
        grid=(block // tile,),
        in_specs=[pl.BlockSpec((rows, width), lambda i: (0, 0))] * len(values)
        + [pl.BlockSpec((pixel.shape[0], tile), lambda i: (0, i)) for pixel in pixels],
        out_specs=[pl.BlockSpec((width // 2, tile), lambda i: (0, i))] * 2,
        out_shape=[half, jax.ShapeDtypeStruct((width // 2, block), bf16)],
        compiler_params=params,
        cost_estimate=cost(2 * rows * len(values) * width * block, *values, *pixels),
        name="sum_images",
    )(*values, *pixels)


def add_parts_kernel(one_ref, two_ref, out_ref):
    total = one_ref[...] + two_ref[...]
    out_ref[...] = total.reshape(out_ref.shape)


def add_parts(one, two, classes):
    width, block = one.shape
    tile = min(block, 2048)
    part = pl.BlockSpec((width, tile), lambda i: (0, i))
    return pl.pallas_call(
        add_parts_kernel,
        grid=(block // tile,),
        in_specs=[part] * 2,
        out_specs=pl.BlockSpec((width // classes, classes, tile), lambda i: (0, 0, i)),
        out_shape=jax.ShapeDtypeStruct((width // classes, classes, block), f32),
        compiler_params=params,
        cost_estimate=cost(2 * width * block, one, two, one),
        name="add_parts",
    )(one, two)


def project_kernel(planes, classes, own_o, depth, order_ref, *refs):
    pieces, (out_ref, prior_ref, tables_ref) = refs[:-3], refs[-3:]
    width = planes * classes
    group = classes * own_o
    taps = depth - 5
    block = pieces[0].shape[1]
    core = order_ref[0] & 1
    lines = -(-depth * group // block)
    for i, piece in enumerate(pieces):
        flat = piece[2 * width :].astype(f32)
        for side in range(2):
            table = []
            for line in range(depth):
                row, column = divmod(line * group, block)
                row += side * lines
                table.append(flat[row : row + 1, column : column + group])
            tables_ref[2 * i + side] = jnp.concatenate(table)
    chip = even_first(tables_ref[0], tables_ref[1], core)
    prior = [jnp.sum(table[taps + 2 :], axis=0, keepdims=True) for table in chip]
    prior_ref[...] = jnp.concatenate(prior, axis=1)
    turned = [turned_taps(table, classes, own_o) for table in chip]
    slices = []
    for i in range(len(pieces)):
        for slab in (order_ref[i], order_ref[i] ^ 1):
            parts = [window(one, slab, planes, taps, classes) for one in turned]
            slices.append(jnp.concatenate(parts, axis=1))
    slices = jnp.concatenate(slices).T.astype(bf16)
    tile = min(block, 512)

    def some(i, energy):
        columns = pl.ds(pl.multiple_of(i * tile, tile), tile)
        stack = jnp.concatenate([piece[: 2 * width, columns] for piece in pieces])
        projection = jnp.dot(slices, stack, preferred_element_type=f32)
        projection = projection.astype(bf16).astype(f32).T
        out_ref[columns] = projection.astype(bf16)
        return energy + jnp.sum(projection * projection, axis=0, keepdims=True)

    energy = lax.fori_loop(0, block // tile, some, jnp.zeros((1, 2 * group), f32))
    high = energy.astype(bf16).astype(f32)
    middle = (energy - high).astype(bf16).astype(f32)
    parts = [high, middle, energy - high - middle, jnp.zeros((13, 2 * group), f32)]
    parts = jnp.concatenate(parts)
    out_ref[block:] = parts.astype(bf16)


def project(order, pieces, planes, classes, own_o, depth):
    block = pieces[0].shape[1]
    group = classes * own_o
    vmem = pl.BlockSpec(memory_space=pltpu.VMEM)
    return pl.pallas_call(
        lambda *refs: project_kernel(planes, classes, own_o, depth, *refs),
        in_specs=[pl.BlockSpec(memory_space=pltpu.SMEM)] + [vmem] * len(pieces),
        out_specs=[vmem] * 3,
        out_shape=[
            jax.ShapeDtypeStruct((block + 16, 2 * group), bf16),
            jax.ShapeDtypeStruct((1, 2 * group), f32),
            jax.ShapeDtypeStruct((2 * len(pieces), depth, group), f32),
        ],
        compiler_params=params,
        cost_estimate=cost(8 * len(pieces) * planes * classes * group * block, *pieces),
        name="project",
    )(order, *pieces)


def match_kernel(order_ref, mine_ref, theirs_ref, *refs):
    pieces, out_ref, pixels_ref = refs[:-2], refs[-2], refs[-1]
    half = mine_ref.shape[0] - 16
    core = order_ref[0] & 1
    exact = pieces[0].shape[0] % 16 == 0
    stack = [piece[...] if exact else piece[...].astype(f32) for piece in pieces]
    pixels_ref[...] = jnp.concatenate(stack).astype(bf16)
    squares = mine_ref[half:].astype(f32) + theirs_ref[half:].astype(f32)
    energy = jnp.sum(squares, axis=0, keepdims=True)
    total = -0.5 * energy
    for side, projection in ((core, mine_ref), (1 - core, theirs_ref)):
        columns = pl.ds(pl.multiple_of(side * half, half), half)
        total += jnp.dot(pixels_ref[:, columns], projection[:half], preferred_element_type=f32)
    out_ref[...] = total.reshape(out_ref.shape)


def match(order, mine, theirs, batches):
    pieces = sum(batches, [])
    rows, block = pieces[0].shape
    rows_all = rows * len(pieces)
    columns = mine.shape[1]
    vmem = pl.BlockSpec(memory_space=pltpu.VMEM)
    return pl.pallas_call(
        match_kernel,
        in_specs=[pl.BlockSpec(memory_space=pltpu.SMEM)] + [vmem] * (2 + len(pieces)),
        out_specs=[vmem] * 2,
        out_shape=[
            jax.ShapeDtypeStruct((len(batches), rows_all // len(batches), columns), f32),
            jax.ShapeDtypeStruct((rows_all, block), bf16),
        ],
        compiler_params=params,
        cost_estimate=cost(2 * rows_all * block * columns, mine, theirs, *pieces),
        name="match",
    )(order, mine, theirs, *pieces)


def pick(blocks, order):
    return jnp.concatenate([lax.dynamic_slice_in_dim(blocks, i, 1) for i in order])


def in_three(value):
    high = lax.reduce_precision(value, 8, 7)
    rest = value - high
    middle = lax.reduce_precision(rest, 8, 7)
    return [part.astype(bf16) for part in (high, middle, rest - middle)]


def local(volumes, band_weights, band_start, images, noise_precision, log_prior):
    planes, classes, block = volumes.shape
    slabs, batches = lax.axis_size("slab"), lax.axis_size("batch")
    slab, batch = lax.axis_index("slab"), lax.axis_index("batch")
    core = slab & 1
    chips = slabs // 2
    own_o, taps = band_weights.shape[1:]
    particles = images.shape[0]
    rows = particles // slabs
    width = planes * classes
    group = classes * own_o
    own_order, other_order = block_orders()

    def part_for(step):
        column = lax.rem(batch + step, batches) * block
        return lax.dynamic_slice(images, (slab * rows, column), (rows, block))

    half = batches // 2
    steps = [step for step in range(1, batches) if step != half]
    steps = steps + [half]
    parts = [part_for(step) for step in steps]
    fetched = [shifted(part, "batch", step) for part, step in zip(parts, steps)]

    coarse = band_start // 128
    table = jnp.concatenate(
        [
            band_weights.reshape(group, taps).T,
            jnp.stack([coarse, band_start - 128 * coarse]).reshape(2, group).astype(bf16),
            jnp.stack(in_three(log_prior)).reshape(3, group),
        ]
    )
    depth = table.shape[0]
    side = block // 2
    extra = -(-table.size // side)
    table = jnp.pad(table.reshape(-1), (0, extra * side - table.size)).reshape(extra, side)
    flat = after(volumes, *parts).reshape(width, block)
    mine = lax.dynamic_slice_in_dim(flat, core * side, side, axis=1)
    give = lax.dynamic_slice_in_dim(flat, (1 - core) * side, side, axis=1)
    theirs = paired(jnp.concatenate([give, table]), (1, 1))
    shard = jnp.concatenate([mine, theirs[:width], table, theirs[width:]])
    shards = spread_start(shard)
    if len(shards) > 1:
        shards[1] = after(shards[1], *fetched[:1])
    shards = spread_end(shards)
    near = []
    for part in fetched[:-1]:
        ties = (near[-1]) if near else (shards[1:])
        near.append(spread_start(after(part, *ties)))
    order = jnp.stack(own_order)
    mine, prior, tables = project(order, shards, planes, classes, own_o, depth)
    held = []
    mine = after(mine, fetched[-1], *sum(near, []))
    theirs = paired(mine, (1, 1))

    later = after(images, mine)
    own = [lax.dynamic_slice(later, (i * rows, batch * block), (rows, block)) for i in own_order]
    total, pixels = match(order, mine, theirs, [own])
    total = total[0]
    pixels = [pixels]
    last = spread_start(fetched[-1])
    for step, each in zip(steps, near):
        part, pixel = match(order, mine, theirs, [spread_end(each)])
        pixels.append(pixel)
        total = total + shifted(part[0], "batch", -step)
    part, pixel = match(order, mine, theirs, [spread_end(last)])
    pixels.append(pixel)
    total = total + shifted(part[0], "batch", -steps[-1])
    total = total.reshape(chips, rows, 2 * group)

    def by_rows(blocks):
        return pick(blocks, chip_places(core))

    noise, prior = lax.optimization_barrier((noise_precision, prior, part))[:2]
    noise = lax.dynamic_index_in_dim(noise.reshape(chips, 2, rows), core, 1, False)
    score = noise[:, :, None] * by_rows(total) + prior
    own_top = jnp.max(score, axis=2)
    shifted_exp = jnp.exp(score - own_top[:, :, None])
    own_total = jnp.sum(shifted_exp, axis=2)
    count = chips * rows
    lines = -(-count // (2 * group))
    sides = jnp.stack(in_three(own_top.reshape(count)) + in_three(own_total.reshape(count)))
    sides = jnp.pad(sides, ((0, 0), (0, lines * 2 * group - count))).reshape(-1, 2 * group)
    packed = jnp.concatenate([shifted_exp.astype(bf16).reshape(count, 2 * group), sides])
    packed = [packed] + [paired(packed, (2 * i, 2 * i)) for i in range(1, chips)]
    packed = jnp.stack(packed)
    exps = packed[:, :count]
    sides = packed[:, count:].reshape(chips, 6, lines * 2 * group)[:, :, :count].astype(f32)
    tops = sides[:, 0] + sides[:, 1] + sides[:, 2]
    totals = sides[:, 3] + sides[:, 4] + sides[:, 5]
    top = jnp.max(tops, axis=0)
    log_evidence = top + jnp.log(jnp.sum(totals * jnp.exp(tops - top), axis=0))
    scale = jnp.exp(tops - log_evidence)
    weights = (exps.astype(f32) * scale[:, :, None]).astype(bf16)

    chip_order = [i // 2 for i in own_order]
    places = list(zip(held_masks(slabs, 0), held_masks(slabs, 1)))
    places = [(even + core * (odd - even)) // 2 for even, odd in places]
    both = pick(window_slices(order, after(tables, part), planes, classes, own_o), places)
    inserted = jnp.einsum("qzo,qno->nz", both, weights, preferred_element_type=f32).astype(bf16)
    inserted = pick(inserted.reshape(chips, rows, 2 * width), chip_order)
    inserted = inserted.reshape(count, 2 * width)
    far = shifted(inserted, "batch", steps[-1])
    there = [inserted] + [shifted(inserted, "batch", step) for step in steps[:-1]] + [far]

    responsibilities = jnp.exp(score.reshape(count, 2 * group) - log_evidence[:, None])
    lines = -(-count // group)
    evidence = jnp.pad(log_evidence, (0, lines * group - count)).reshape(lines, group)
    halves = even_first(responsibilities[:, :group], responsibilities[:, group:], core)
    mine = jnp.concatenate([halves[0], evidence])
    theirs = paired(jnp.concatenate([halves[1], evidence]), (1, 1))

    def in_order(one, two):
        return jnp.stack(even_first(one, two, core), axis=1)

    responsibilities = in_order(
        mine[:count].reshape(chips, rows, group), theirs[:count].reshape(chips, rows, group)
    ).reshape(particles, group)
    evidence = [each[count:].reshape(-1)[:count].reshape(chips, rows) for each in (mine, theirs)]
    log_evidence = in_order(*evidence).reshape(particles)

    there[0] = after(there[0], theirs)
    keep, give = sum_images(there, pixels)
    backprojection = add_parts(keep, paired(give, (1, 1)), classes)
    return (
        responsibilities.T.reshape(classes, own_o, particles),
        log_evidence,
        backprojection,
    )


def solution(mesh):
    in_specs = (
        P("slab", None, "batch"),
        P(None, "slab", None),
        P(None, "slab"),
        P("batch", None),
        P("batch"),
        P(None, "slab"),
    )
    out_specs = (P(None, "slab", "batch"), P("batch"), P("slab", None, "batch"))
    return jax.shard_map(local, mesh=mesh, in_specs=in_specs, out_specs=out_specs, check_vma=False)
```
